32 devices in a mesh: frame: 4 (over z), pos: 8 (over y, x, core).
Axes of the slice: x: 2, y: 2, z: 4, core: 2. Of those that a mesh axis runs over, the one named last changes fastest.
Arguments:
- latents: bfloat16 [128, 512, 256], P('frame', 'pos'), as said below
- gain_one: float32 [256], replicated, may hold values from 0.5 to 1.5
- query_one: bfloat16 [256, 256], replicated, as said below
- key_one: bfloat16 [256, 256], replicated, as said below
- value_one: bfloat16 [256, 256], replicated, may hold values from -0.375 to 0.375
- out_one: bfloat16 [256, 256], replicated, may hold values from -0.75 to 0.75
- gain_two: float32 [256], replicated, may hold values from 0.5 to 1.5
- query_two: bfloat16 [256, 256], replicated, as said below
- key_two: bfloat16 [256, 256], replicated, as said below
- value_two: bfloat16 [256, 256], replicated, may hold values from -0.375 to 0.375
- out_two: bfloat16 [256, 256], replicated, may hold values from -0.75 to 0.75
Outputs:
- decoded: bfloat16 [128, 512, 256], P('frame', 'pos')
The draws below stay inside these ranges and needn't reach their ends.
Inputs may be any that keep to these rules, and one draw needn't show every extreme that they name: `latents`: latent features of the video. `query_one`: A projection of the spatial block. `key_one`: A projection of the spatial block. `query_two`: A projection of the temporal block. `key_two`: A projection of the temporal block.
All inputs are finite; a program needn't handle non-finite values.
Results may differ from the reference program's by a relative error of at most 0.015.
The reference program's roundings to bfloat16 on the way count: a program that leaves them out, or rounds other values in their place, can miss the bound.
Values may be sent and summed in bfloat16 or wider, within the bound.
No kernel may reach another device: no remote copies, remote signals or barrier semaphores. Data moves between devices by JAX's collectives and lax.ppermute only.
A program may use at most 320 MiB of HBM per device.

```python
import math
import jax
import jax.numpy as jnp
from jax import lax

C = 256
HEADS = 4
HEAD_DIM = 64
FRAMES = 128
POSITIONS = 512


def draw_latents(key, part):
    return jax.random.normal(jax.random.fold_in(key, 102), (FRAMES, POSITIONS, C), jnp.float32).astype(jnp.bfloat16)


def attention_weight(key, salt):
    noise = jax.random.normal(jax.random.fold_in(key, salt), (C, C), jnp.float32)
    return (noise * (1.5 / math.sqrt(C))).astype(jnp.bfloat16)


def draw_query_one(key, part):
    return attention_weight(key, 201)


def draw_key_one(key, part):
    return attention_weight(key, 202)


def draw_query_two(key, part):
    return attention_weight(key, 203)


def draw_key_two(key, part):
    return attention_weight(key, 204)


def bell_draw(key, shape, spread, limit, kind=jnp.bfloat16):
    entries = jax.random.normal(key, shape, jnp.float32) * spread
    return jnp.minimum(jnp.maximum(entries, -limit), limit).astype(kind)


def setup_inputs(seed: int = 0) -> dict:
    key_of = jax.random.split(jax.random.key(seed), 12)
    return {
        "latents": draw_latents(jax.random.fold_in(key_of[11], 71), 0),
        "gain_one": jnp.clip(1.0 + 0.1 * jax.random.normal(key_of[1], (C,), jnp.float32), 0.5, 1.5),
        "query_one": draw_query_one(jax.random.fold_in(key_of[11], 71), 0),
        "key_one": draw_key_one(jax.random.fold_in(key_of[11], 71), 0),
        "value_one": bell_draw(key_of[4], (C, C), C ** -0.5, 0.375),
        "out_one": bell_draw(key_of[5], (C, C), (C // 4) ** -0.5, 0.75),
        "gain_two": jnp.clip(1.0 + 0.1 * jax.random.normal(key_of[6], (C,), jnp.float32), 0.5, 1.5),
        "query_two": draw_query_two(jax.random.fold_in(key_of[11], 71), 0),
        "key_two": draw_key_two(jax.random.fold_in(key_of[11], 71), 0),
        "value_two": bell_draw(key_of[9], (C, C), C ** -0.5, 0.375),
        "out_two": bell_draw(key_of[10], (C, C), (C // 4) ** -0.5, 0.75),
    }


def normed(values, gain):
    wide = values.astype(jnp.float32)
    factor = lax.rsqrt(lax.optimization_barrier(jnp.mean(wide * wide, axis=-1, keepdims=True)) + 1e-06)
    return (wide * factor * gain).astype(jnp.bfloat16)

def project(values, weight):
    flat = values.reshape(-1, values.shape[-1])
    result = jnp.dot(flat, weight, preferred_element_type=jnp.float32).astype(jnp.bfloat16)
    return result.reshape(values.shape[:-1] + (weight.shape[1],))

def heads_of(values):
    return values.reshape(values.shape[:-1] + (HEADS, HEAD_DIM))

def rounded_weights(weights):
    return lax.optimization_barrier(weights.astype(jnp.bfloat16)).astype(jnp.float32)

def reference(latents, gain_one, query_one, key_one, value_one, out_one, gain_two, query_two, key_two, value_two, out_two):
    scale = HEAD_DIM ** (-0.5)
    normed_one = normed(latents, gain_one)
    q_one = heads_of(project(normed_one, query_one))
    k_one = heads_of(project(normed_one, key_one))
    v_one = heads_of(project(normed_one, value_one))

    def spatial(index):
        query = q_one[index].astype(jnp.float32)
        keys = jnp.concatenate([k_one[index], k_one[0]], axis=0).astype(jnp.float32)
        vals = jnp.concatenate([v_one[index], v_one[0]], axis=0).astype(jnp.float32)
        scores = jnp.einsum('phd,khd->hpk', query, keys) * scale
        weights = jnp.exp(scores - lax.optimization_barrier(jnp.max(scores, axis=-1, keepdims=True)))
        totals = lax.optimization_barrier(jnp.sum(weights, axis=-1))
        summed = jnp.einsum('hpk,khd->phd', rounded_weights(weights), vals)
        return (summed / totals.T[:, :, None]).reshape(POSITIONS, C).astype(jnp.bfloat16)
    attended_one = lax.map(spatial, jnp.arange(FRAMES, dtype=jnp.int32))
    mid = (latents.astype(jnp.float32) + jnp.dot(attended_one.reshape(-1, C), out_one, preferred_element_type=jnp.float32).reshape(FRAMES, POSITIONS, C)).astype(jnp.bfloat16)
    normed_two = normed(mid, gain_two)
    q_two = heads_of(project(normed_two, query_two)).transpose(1, 0, 2, 3)
    k_two = heads_of(project(normed_two, key_two)).transpose(1, 0, 2, 3)
    v_two = heads_of(project(normed_two, value_two)).transpose(1, 0, 2, 3)

    def temporal(operands):
        query, keys, vals = operands
        scores = jnp.einsum('fhd,khd->hfk', query.astype(jnp.float32), keys.astype(jnp.float32)) * scale
        weights = jnp.exp(scores - lax.optimization_barrier(jnp.max(scores, axis=-1, keepdims=True)))
        totals = lax.optimization_barrier(jnp.sum(weights, axis=-1))
        summed = jnp.einsum('hfk,khd->fhd', rounded_weights(weights), vals.astype(jnp.float32))
        return (summed / totals.T[:, :, None]).reshape(FRAMES, C).astype(jnp.bfloat16)
    attended_two = lax.map(temporal, (q_two, k_two, v_two)).transpose(1, 0, 2)
    mixed = jnp.dot(attended_two.reshape(-1, C), out_two, preferred_element_type=jnp.float32).reshape(FRAMES, POSITIONS, C)
    return (mid.astype(jnp.float32) + mixed).astype(jnp.bfloat16)
```

```python
import functools

import jax
import jax.numpy as jnp
from jax import lax
from jax.experimental import pallas as pl
from jax.experimental.pallas import tpu as pltpu
from jax.sharding import PartitionSpec as P

HEADS = 4
LANES = 128
LOG2E = 1.4426950408889634


def normed(wide, gain):
    factor = lax.rsqrt(jnp.mean(wide * wide, axis=-1, keepdims=True) + 1e-06)
    return (wide * factor * gain).astype(jnp.bfloat16)


def dot(left, right):
    return jnp.dot(left, right, preferred_element_type=jnp.float32)


def dot_t(left, right):
    return lax.dot_general(
        left, right, (((1,), (1,)), ((), ())), preferred_element_type=jnp.float32
    )


def head_mask(rows, width, head):
    depth = width // HEADS
    lane = lax.broadcasted_iota(jnp.int32, (rows, width), 1)
    return (lane >= head * depth) & (lane < (head + 1) * depth)


def spatial_kernel(
    chips, shards, zf_ref, *refs
):
    mine, refs = refs[:chips], refs[chips:]
    other, refs = refs[:chips], refs[chips:]
    x0_ref, gain_ref, wq_ref, wk_ref, wv_ref, wo_ref = refs[:6]
    outs = refs[6 : 6 + shards]
    k_s, v_s, mid_s = refs[6 + shards :]
    width = wq_ref.shape[0]
    depth = width // HEADS
    half = width // 2
    gain = gain_ref[...]
    places = x0_ref.shape[0]
    local = mine[0].shape[1]

    @pl.when(pl.program_id(0) == 0)
    def _():
        n0 = normed(x0_ref[...].astype(jnp.float32), gain)
        k_s[places:, :] = dot(n0, wk_ref[...]).astype(jnp.bfloat16)
        v0 = dot(n0, wv_ref[...]).astype(jnp.bfloat16)
        ones = jnp.ones((2 * places, half), jnp.bfloat16)
        for pair in range(2):
            v_s[pair, places:, :half] = v0[:, pair * half : (pair + 1) * half]
            v_s[pair, :, half:] = ones

    x_mine = jnp.concatenate([r[0] for r in mine], axis=0).astype(jnp.float32)
    x_other = jnp.concatenate([r[0] for r in other], axis=0).astype(jnp.float32)
    n_mine = normed(x_mine, gain)
    n_all = jnp.concatenate([n_mine, normed(x_other, gain)], axis=0)
    k_s[:places, :] = dot(n_all, wk_ref[...]).astype(jnp.bfloat16)
    v = dot(n_all, wv_ref[...]).astype(jnp.bfloat16)
    for pair in range(2):
        v_s[pair, :places, :half] = v[:, pair * half : (pair + 1) * half]
    q = dot(n_mine, wq_ref[...]).astype(jnp.bfloat16)
    rows = q.shape[0]
    low = lax.broadcasted_iota(jnp.int32, (rows, half), 1) < depth
    keys = k_s[...]
    parts = []
    for pair in range(2):
        res = []
        for head in (2 * pair, 2 * pair + 1):
            qm = jnp.where(head_mask(rows, width, head), q, jnp.zeros_like(q))
            s = dot_t(qm, keys)
            m = jnp.max(s, axis=-1, keepdims=True)
            w = jnp.exp2((s - m) * (depth**-0.5 * LOG2E)).astype(jnp.bfloat16)
            res.append(dot(w, v_s[pair]))
        top = jnp.where(low, res[0][:, :half], res[1][:, :half])
        bottom = jnp.where(low, res[0][:, half:], res[1][:, half:])
        parts.append(top / bottom)
    attended = jnp.concatenate(parts, axis=1).astype(jnp.bfloat16)
    mid_s[...] = x_mine + dot(attended, wo_ref[...])
    zf = zf_ref[0]
    share = local // shards
    for t in range(shards):
        for s in range(chips):
            at = pl.multiple_of(s * local + (t ^ zf) * share, share)
            outs[t][s, 0] = mid_s[pl.ds(at, share), :].astype(jnp.bfloat16)


def spatial(zf, mine, other, x0, gain, wq, wk, wv, wo, shards):
    chips = len(mine)
    frames, local, width = mine[0].shape
    places = x0.shape[0]
    share = local // shards
    piece = pl.BlockSpec((1, local, width), lambda f, z: (f, 0, 0))
    full = lambda a: pl.BlockSpec(a.shape, lambda f, z, n=a.ndim: (0,) * n)
    return pl.pallas_call(
        functools.partial(spatial_kernel, chips, shards),
        grid_spec=pltpu.PrefetchScalarGridSpec(
            num_scalar_prefetch=1,
            grid=(frames,),
            in_specs=[piece] * (2 * chips) + [full(a) for a in (x0, gain, wq, wk, wv, wo)],
            out_specs=[pl.BlockSpec((chips, 1, share, width), lambda f, z: (0, f, 0, 0))] * shards,
            scratch_shapes=[
                pltpu.VMEM((2 * places, width), jnp.bfloat16),
                pltpu.VMEM((2, 2 * places, width), jnp.bfloat16),
                pltpu.VMEM((chips * local, width), jnp.float32),
            ],
        ),
        out_shape=[jax.ShapeDtypeStruct((chips, frames, share, width), jnp.bfloat16)] * shards,
        compiler_params=pltpu.CompilerParams(vmem_limit_bytes=48 * 2**20),
        name="spatial",
    )(zf, *mine, *other, x0, gain, wq, wk, wv, wo)


def take(ref, rows):
    return jnp.concatenate([ref[i, rows, :] for i in range(ref.shape[0])], axis=1)


def put(ref, rows, value):
    for i in range(ref.shape[0]):
        ref[i, rows, :] = value[:, i * LANES : (i + 1) * LANES]


def temporal_kernel(chips, shards, share, *refs):
    own, refs = refs[:shards], refs[shards:]
    came, refs = refs[: chips - 1], refs[chips - 1 :]
    gain_ref, wq_ref, wk_ref, wv_ref, wo_ref = refs[:5]
    outs = refs[5 : 5 + shards]
    x_s, q_s, k_s, v_s, a_s = refs[5 + shards :]
    width = wq_ref.shape[0]
    depth = width // HEADS
    half = width // 2
    block = own[0].shape[0]
    frames = block // share * chips * shards
    for t in range(shards):
        for s in range(chips):
            piece = own[t][...] if s == 0 else came[s - 1][t]
            put(x_s, pl.ds((t * chips + s) * block, block), piece.astype(jnp.float32))
    gain = gain_ref[...]
    for p in range(share):
        n = normed(take(x_s, pl.ds(p, frames, stride=share)), gain)
        q_s[p] = dot(n, wq_ref[...]).astype(jnp.bfloat16)
        k_s[p] = dot(n, wk_ref[...]).astype(jnp.bfloat16)
        v_s[p] = dot(n, wv_ref[...]).astype(jnp.bfloat16)
    lane = lax.broadcasted_iota(jnp.int32, (frames, half), 1)
    low, high = lane < depth, lane >= depth
    ones = [c.astype(jnp.float32).astype(jnp.bfloat16) for c in (low, high)]

    for p in range(share):
        q, k, v = q_s[p], k_s[p], v_s[p]
        parts = []
        for pair in range(2):
            cols = slice(pair * half, (pair + 1) * half)
            zero = jnp.zeros((frames, half), jnp.bfloat16)
            kp, vp = k[:, cols], v[:, cols]
            k2 = jnp.concatenate([jnp.where(low, kp, zero), jnp.where(high, kp, zero)], axis=0)
            v2 = jnp.concatenate(
                [
                    jnp.concatenate([jnp.where(low, vp, zero), ones[0]], axis=1),
                    jnp.concatenate([jnp.where(high, vp, zero), ones[1]], axis=1),
                ],
                axis=0,
            )
            s = dot_t(q[:, cols], k2)
            m0 = jnp.max(s[:, :frames], axis=-1, keepdims=True)
            m1 = jnp.max(s[:, frames:], axis=-1, keepdims=True)
            c = depth**-0.5 * LOG2E
            w = jnp.concatenate(
                [jnp.exp2((s[:, :frames] - m0) * c), jnp.exp2((s[:, frames:] - m1) * c)], axis=1
            ).astype(jnp.bfloat16)
            r = dot(w, v2)
            parts.append(r[:, :half] / r[:, half:])
        a = jnp.concatenate(parts, axis=1).astype(jnp.bfloat16)
        rows = pl.ds(p, frames, stride=share)
        put(a_s, rows, take(x_s, rows) + dot(a, wo_ref[...]))
    for t in range(shards):
        for s in range(chips):
            outs[t][s] = take(a_s, pl.ds((t * chips + s) * block, block)).astype(jnp.bfloat16)


def temporal(own, came, gain, wq, wk, wv, wo, share):
    shards, chips = len(own), len(came) + 1
    block, width = own[0].shape
    rows = block * chips * shards
    frames = rows // share
    return pl.pallas_call(
        functools.partial(temporal_kernel, chips, shards, share),
        out_shape=[jax.ShapeDtypeStruct((chips, block, width), jnp.bfloat16)] * shards,
        scratch_shapes=[
            pltpu.VMEM((width // LANES, rows, LANES), jnp.float32),
            pltpu.VMEM((share, frames, width), jnp.bfloat16),
            pltpu.VMEM((share, frames, width), jnp.bfloat16),
            pltpu.VMEM((share, frames, width), jnp.bfloat16),
            pltpu.VMEM((width // LANES, rows, LANES), jnp.float32),
        ],
        compiler_params=pltpu.CompilerParams(vmem_limit_bytes=48 * 2**20),
        name="temporal",
    )(*own, *came, gain, wq, wk, wv, wo)


def assemble_kernel(shards, share, ids_ref, *refs):
    pieces, out_ref, wide = refs[:shards], refs[shards], refs[shards + 1]
    for t in range(shards):
        at = pl.multiple_of((t ^ ids_ref[0]) * share, share)
        wide[:, pl.ds(at, share), :] = pieces[t][0].astype(jnp.float32)
    out_ref[...] = wide[...].astype(jnp.bfloat16)


def assemble(ids, pieces):
    shards = len(pieces)
    chips, frames, share, width = pieces[0].shape
    return pl.pallas_call(
        functools.partial(assemble_kernel, shards, share),
        grid_spec=pltpu.PrefetchScalarGridSpec(
            num_scalar_prefetch=1,
            grid=(chips,),
            in_specs=[pl.BlockSpec((1, frames, share, width), lambda s, ids: (s, 0, 0, 0))] * shards,
            out_specs=pl.BlockSpec(
                (frames, shards * share, width), lambda s, ids: (s ^ ids[1], 0, 0)
            ),
            scratch_shapes=[pltpu.VMEM((frames, shards * share, width), jnp.float32)],
        ),
        out_shape=jax.ShapeDtypeStruct((chips * frames, shards * share, width), jnp.bfloat16),
        name="assemble",
    )(ids, *pieces)


def swap(value, axis, size, mask):
    return lax.ppermute(value, axis, [(i, i ^ mask) for i in range(size)])


def shards_fn(
    shards,
    spots,
    latents,
    gain_one,
    query_one,
    key_one,
    value_one,
    out_one,
    gain_two,
    query_two,
    key_two,
    value_two,
    out_two,
):
    frames, local, width = latents.shape
    chips = spots // 2
    each = frames // chips
    share = local // shards
    zf = lax.axis_index("frame")
    chip = lax.axis_index("pos") // 2
    ids = jnp.stack([zf, chip]).astype(jnp.int32)

    first = latents[0]
    found = first
    for s in range(1, shards):
        sent = lax.ppermute(first, "frame", [(0, s)])
        found = jnp.where(zf == s, sent, found)
    x0 = lax.all_gather(found, "pos", axis=0, tiled=True)

    mine = [lax.dynamic_slice_in_dim(latents, (chip ^ s) * each, each, 0) for s in range(chips)]
    mine = [mine[0]] + [swap(mine[s], "pos", spots, 2 * s) for s in range(1, chips)]
    other = [swap(m, "pos", spots, 1) for m in mine]
    row = lambda g: g.reshape(1, -1)
    mid = spatial(
        ids, mine, other, x0, row(gain_one), query_one, key_one, value_one, out_one, shards
    )
    mid = [mid[0]] + [swap(mid[t], "frame", shards, t) for t in range(1, shards)]
    flat = [m.reshape(chips, each * share, width) for m in mid]
    own = [m[0] for m in flat]
    came = [
        swap(jnp.stack([m[s] for m in flat]), "pos", spots, 2 * s) for s in range(1, chips)
    ]
    done = temporal(
        own, came, row(gain_two), query_two, key_two, value_two, out_two, share
    )
    done = [done[0]] + [swap(done[t], "frame", shards, t) for t in range(1, shards)]
    return assemble(ids, [d.reshape(chips, each, share, width) for d in done])


def solution(mesh):
    return jax.shard_map(
        functools.partial(shards_fn, mesh.shape["frame"], mesh.shape["pos"]),
        mesh=mesh,
        in_specs=(P("frame", "pos", None), P(), P(), P(), P(), P(), P(), P(), P(), P(), P()),
        out_specs=P("frame", "pos", None),
        check_vma=False,
    )
```

```python
import functools

import jax
import jax.numpy as jnp
from jax import lax
from jax.experimental import pallas as pl
from jax.experimental.pallas import tpu as pltpu
from jax.sharding import PartitionSpec as P

HEADS = 4
LANES = 128
EARLY = 40
SPLIT = 8
LATER = 6.4
ROOM = 26 * 2**20
TURNS = 2
LOG2E = 1.4426950408889634


def normed(wide, gain):
    factor = lax.rsqrt(jnp.mean(wide * wide, axis=-1, keepdims=True) + 1e-06)
    return wide * factor * gain


def dot(left, right):
    return jnp.dot(left, right, preferred_element_type=jnp.float32)


def dot_t(left, right):
    return lax.dot_general(
        left, right, (((1,), (1,)), ((), ())), preferred_element_type=jnp.float32
    )


def project(mine, other, gain_ref, wq_ref, wk_ref, wv_ref, q_ref, k_ref, v_ref, turns):
    chips = len(mine)
    local, width = mine[0].shape[1:]
    asked, frames = q_ref.shape[0], k_ref.shape[0]
    gain = gain_ref[...]
    rows = [r[:frames] for r in mine] + [other[s] for s in range(chips)]
    normal = [normed(r.reshape(frames * local, width).astype(jnp.float32), gain) for r in rows]
    short = [n.astype(jnp.bfloat16) for n in normal]
    for weight, out in ((wk_ref, k_ref), (wv_ref, v_ref)):
        for s in range(2 * chips):
            got = dot(short[s], weight[...]).astype(jnp.bfloat16)
            out[:, s * local : (s + 1) * local, :] = got.reshape(frames, local, width)
    scale = (width // HEADS) ** -0.5 * LOG2E
    wide = [n.reshape(frames, local, width) for n in normal[:chips]]
    for f in range(asked):
        n = jnp.concatenate([w[f] for w in wide], axis=0)
        n = jnp.concatenate([pick(n, chips, turns, j) for j in range(turns)], axis=0)
        q_ref[f] = (dot(n.astype(jnp.bfloat16), wq_ref[...]) * scale).astype(jnp.bfloat16)


def pick(rows, chips, turns, turn):
    local = rows.shape[0] // chips
    run = local // turns
    return jnp.concatenate(
        [rows[s * local + turn * run : s * local + (turn + 1) * run] for s in range(chips)], axis=0
    )


def attend(turns, turn, zf, parts, wo_ref, outs, mid_s, by_shard):
    chips = len(parts[0][0])
    shards = len(outs) * outs[0].shape[0] // chips
    step, width = outs[0].shape[2:]
    half = width // 2
    depth = width // HEADS
    rows = chips * shards * step
    k0, v0 = parts[-1][2], parts[-1][3]
    last = k0.shape[0] - 1
    places = k0.shape[1]
    low = lax.broadcasted_iota(jnp.int32, (rows, half), 1) < depth
    ones = jnp.ones((2 * places, half), jnp.bfloat16)
    frames = [(part, f) for part in parts for f in range(part[1].shape[0])]
    together = max(1, min(len(frames), ROOM // (2 * (2 * rows) * (2 * places) * 6)))
    for start in range(0, len(frames), together):
        now = frames[start : start + together]
        items = [(part, f, slice(p * half, (p + 1) * half)) for part, f in now for p in range(2)]
        scores = []
        for (_, q_ref, k_ref, _), f, cols in items:
            q = q_ref[f, turn * rows : (turn + 1) * rows, cols]
            zero = jnp.zeros_like(q)
            q = jnp.concatenate([jnp.where(low, q, zero), jnp.where(low, zero, q)], axis=0)
            scores.append(dot_t(q, jnp.concatenate([k_ref[f, :, cols], k0[last, :, cols]], axis=0)))
        weights = [
            jnp.exp2(s - jnp.max(s, axis=-1, keepdims=True)).astype(jnp.bfloat16) for s in scores
        ]
        sums = []
        for w, ((_, _, _, v_ref), f, cols) in zip(weights, items):
            vals = jnp.concatenate([v_ref[f, :, cols], v0[last, :, cols]], axis=0)
            r = dot(w, jnp.concatenate([vals, ones], axis=1))
            top = jnp.where(low, r[:rows, :half], r[rows:, :half])
            bottom = jnp.where(low, r[:rows, half:], r[rows:, half:])
            sums.append(top / bottom)
        for u, ((pieces, *_), f) in enumerate(now):
            a = jnp.concatenate(sums[2 * u : 2 * u + 2], axis=1).astype(jnp.bfloat16)
            x = jnp.concatenate([r[f].astype(jnp.float32) for r in pieces], axis=0)
            mid_s[start + u] = pick(x, chips, turns, turn) + dot(a, wo_ref[...])
    for f in range(len(frames)):
        for t in range(shards):
            for s in range(chips):
                at = pl.multiple_of((s * shards + (t ^ zf)) * step, step)
                piece = mid_s[f, pl.ds(at, step), :].astype(jnp.bfloat16)
                if by_shard:
                    outs[t][s, f] = piece
                else:
                    outs[s][t, f] = piece


def early_kernel(chips, turns, *refs):
    mine, (other, gain, wq, wk, wv, q, k, v) = refs[:chips], refs[chips:]
    project(mine, other, gain, wq, wk, wv, q, k, v, turns)


def first_kernel(chips, shards, turns, ids_ref, *refs):
    early, refs = refs[:chips], refs[chips:]
    late, refs = refs[:chips], refs[chips:]
    other, gain, wq, wk, wv, wo, q1, k1, v1 = refs[:9]
    outs, (q2, k2, v2, mid_s) = refs[9 : 9 + shards], refs[9 + shards :]
    project(late, other, gain, wq, wk, wv, q2, k2, v2, turns)
    attend(turns, 0, ids_ref[0], [(early, q1, k1, v1), (late, q2, k2, v2)], wo, outs, mid_s, True)


def later_kernel(chips, shards, turns, turn, ids_ref, *refs):
    early, refs = refs[:chips], refs[chips:]
    late, refs = refs[:chips], refs[chips:]
    q1, k1, v1, q2, k2, v2, wo = refs[:7]
    outs, mid_s = refs[7:-1], refs[-1]
    attend(turns, turn, ids_ref[0], [(early, q1, k1, v1), (late, q2, k2, v2)], wo, outs, mid_s, False)


def vmem(count):
    return [pl.BlockSpec(memory_space=pltpu.VMEM)] * count


def cost(microseconds):
    return pl.CostEstimate(
        flops=int(microseconds * 1e9), bytes_accessed=int(microseconds * 3.6e6), transcendentals=0
    )


def params():
    return pltpu.CompilerParams(vmem_limit_bytes=40 * 2**20)


def shape(*sizes):
    return jax.ShapeDtypeStruct(sizes, jnp.bfloat16)


def saved_shapes(frames, asked, local, chips, width):
    return [
        shape(asked, chips * local, width),
        shape(frames, 2 * chips * local, width),
        shape(frames, 2 * chips * local, width),
    ]


def spatial_early(mine, other, gain, wq, wk, wv, shards, turns):
    chips = len(mine)
    frames, local, width = other.shape[1:]
    args = (*mine, other, gain, wq, wk, wv)
    return pl.pallas_call(
        functools.partial(early_kernel, chips, turns),
        in_specs=vmem(len(args)),
        out_specs=vmem(3),
        out_shape=saved_shapes(frames, frames, local, chips, width),
        compiler_params=params(),
        cost_estimate=cost(EARLY),
        name="spatial_early",
    )(*args)


def spatial_first(ids, early, late, other, gain, wq, wk, wv, wo, saved, shards, turns):
    chips = len(early)
    local, width = early[0].shape[1:]
    frames, extra = saved[0].shape[0], late[0].shape[0]
    step = local // shards // turns
    total = frames + extra - 1
    args = (*early, *late, other, gain, wq, wk, wv, wo, *saved)
    out = [shape(chips, total, step, width)] * shards
    out = out + saved_shapes(extra, extra - 1, local, chips, width)
    got = pl.pallas_call(
        functools.partial(first_kernel, chips, shards, turns),
        in_specs=[pl.BlockSpec(memory_space=pltpu.SMEM)] + vmem(len(args)),
        out_specs=vmem(len(out)),
        out_shape=out,
        scratch_shapes=[pltpu.VMEM((total, chips * shards * step, width), jnp.float32)],
        compiler_params=params(),
        cost_estimate=cost(7.5),
        name="spatial_first",
    )(ids, *args)
    return got[:shards], got[shards:]


def spatial_later(ids, early, late, saved, wo, shards, turns, turn):
    chips = len(early)
    local, width = early[0].shape[1:]
    total = saved[0].shape[0] + saved[3].shape[0]
    step = local // shards // turns
    args = (*early, *late, *saved, wo)
    return pl.pallas_call(
        functools.partial(later_kernel, chips, shards, turns, turn),
        in_specs=[pl.BlockSpec(memory_space=pltpu.SMEM)] + vmem(len(args)),
        out_specs=vmem(chips),
        out_shape=[shape(shards, total, step, width)] * chips,
        scratch_shapes=[pltpu.VMEM((total, chips * shards * step, width), jnp.float32)],
        compiler_params=params(),
        cost_estimate=cost(LATER),
        name="spatial_later",
    )(ids, *args)


def take(ref, rows):
    return jnp.concatenate([ref[i, rows, :] for i in range(ref.shape[0])], axis=1)


def put(ref, rows, value):
    for i in range(ref.shape[0]):
        ref[i, rows, :] = value[:, i * LANES : (i + 1) * LANES]


def temporal_kernel(chips, shards, share, by_shard, *refs):
    near, far = (shards, chips) if by_shard else (chips, shards)
    own, refs = refs[:near], refs[near:]
    came, refs = refs[: far - 1], refs[far - 1 :]
    gain_ref, wq_ref, wk_ref, wv_ref, wo_ref = refs[:5]
    outs = refs[5 : 5 + shards]
    x_s, q_s, k_s, v_s, a_s = refs[5 + shards :]
    width = wq_ref.shape[0]
    depth = width // HEADS
    half = width // 2
    block = own[0].shape[0]
    frames = block // share * chips * shards
    for t in range(shards):
        for s in range(chips):
            i, j = (t, s) if by_shard else (s, t)
            piece = own[i][...] if j == 0 else came[j - 1][i]
            put(x_s, pl.ds((t * chips + s) * block, block), piece.astype(jnp.float32))
    gain = gain_ref[...]
    for p in range(share):
        n = normed(take(x_s, pl.ds(p, frames, stride=share)), gain).astype(jnp.bfloat16)
        q_s[p] = (dot(n, wq_ref[...]) * (depth**-0.5 * LOG2E)).astype(jnp.bfloat16)
        k_s[p] = dot(n, wk_ref[...]).astype(jnp.bfloat16)
        v_s[p] = dot(n, wv_ref[...]).astype(jnp.bfloat16)
    lane = lax.broadcasted_iota(jnp.int32, (frames, half), 1)
    low, high = lane < depth, lane >= depth
    ones = [c.astype(jnp.float32).astype(jnp.bfloat16) for c in (low, high)]

    zero = jnp.zeros((frames, half), jnp.bfloat16)
    items = [(p, slice(i * half, (i + 1) * half)) for p in range(share) for i in range(2)]
    scores = []
    for p, cols in items:
        k = k_s[p, :, cols]
        k = jnp.concatenate([jnp.where(low, k, zero), jnp.where(high, k, zero)], axis=0)
        scores.append(dot_t(q_s[p, :, cols], k))
    weights = []
    for s in scores:
        tops = [jnp.max(s[:, i * frames : (i + 1) * frames], axis=-1, keepdims=True) for i in range(2)]
        w = [jnp.exp2(s[:, i * frames : (i + 1) * frames] - tops[i]) for i in range(2)]
        weights.append(jnp.concatenate(w, axis=1).astype(jnp.bfloat16))
    parts = []
    for w, (p, cols) in zip(weights, items):
        v = v_s[p, :, cols]
        v = jnp.concatenate(
            [
                jnp.concatenate([jnp.where(low, v, zero), ones[0]], axis=1),
                jnp.concatenate([jnp.where(high, v, zero), ones[1]], axis=1),
            ],
            axis=0,
        )
        r = dot(w, v)
        parts.append(r[:, :half] / r[:, half:])
    for p in range(share):
        a = jnp.concatenate(parts[2 * p : 2 * p + 2], axis=1).astype(jnp.bfloat16)
        rows = pl.ds(p, frames, stride=share)
        put(a_s, rows, take(x_s, rows) + dot(a, wo_ref[...]))
    for t in range(shards):
        for s in range(chips):
            outs[t][s] = take(a_s, pl.ds((t * chips + s) * block, block)).astype(jnp.bfloat16)


def temporal(own, came, gain, wq, wk, wv, wo, share, by_shard):
    shards, chips = len(own), len(came) + 1
    if not by_shard:
        shards, chips = chips, shards
    block, width = own[0].shape
    rows = block * chips * shards
    frames = rows // share
    return pl.pallas_call(
        functools.partial(temporal_kernel, chips, shards, share, by_shard),
        out_shape=[jax.ShapeDtypeStruct((chips, block, width), jnp.bfloat16)] * shards,
        scratch_shapes=[
            pltpu.VMEM((width // LANES, rows, LANES), jnp.float32),
            pltpu.VMEM((share, frames, width), jnp.bfloat16),
            pltpu.VMEM((share, frames, width), jnp.bfloat16),
            pltpu.VMEM((share, frames, width), jnp.bfloat16),
            pltpu.VMEM((width // LANES, rows, LANES), jnp.float32),
        ],
        compiler_params=pltpu.CompilerParams(vmem_limit_bytes=48 * 2**20),
        cost_estimate=cost(1.9),
        name="temporal",
    )(*own, *came, gain, wq, wk, wv, wo)


def assemble_kernel(turn, ids_ref, *refs):
    shards = len(refs) - 4
    pieces, (_, out_ref, held, sem) = refs[:shards], refs[shards:]
    chips, frames, step, _ = pieces[0].shape
    run = shards * step
    for z in range(shards):

        @pl.when(ids_ref[0] == z)
        def _():
            for s in range(chips):
                got = [pieces[g ^ z][s].astype(jnp.float32) for g in range(shards)]
                held[pl.ds((s ^ ids_ref[1]) * frames, frames)] = jnp.concatenate(got, axis=1).astype(
                    jnp.bfloat16
                )

    copy = pltpu.make_async_copy(held, out_ref.at[:, pl.ds(turn * run, run), :], sem)
    copy.start()
    copy.wait()


def assemble(ids, pieces, whole, turn):
    shards = len(pieces)
    chips, frames, step, width = pieces[0].shape
    return pl.pallas_call(
        functools.partial(assemble_kernel, turn),
        in_specs=[pl.BlockSpec(memory_space=pltpu.SMEM)]
        + vmem(shards)
        + [pl.BlockSpec(memory_space=pl.ANY)],
        out_specs=pl.BlockSpec(memory_space=pl.ANY),
        out_shape=jax.ShapeDtypeStruct(whole.shape, whole.dtype),
        scratch_shapes=[
            pltpu.VMEM((chips * frames, shards * step, width), jnp.bfloat16),
            pltpu.SemaphoreType.DMA(()),
        ],
        input_output_aliases={shards + 1: 0},
        compiler_params=params(),
        cost_estimate=cost(60 if turn == 0 else 1),
        name="assemble",
    )(ids, *pieces, whole)


def blank(sizes):
    return pl.pallas_call(
        lambda out_ref: None,
        out_specs=pl.BlockSpec(memory_space=pl.ANY),
        out_shape=shape(*sizes),
        name="blank",
    )()


def swap(value, axis, size, mask):
    return lax.ppermute(value, axis, [(i, i ^ mask) for i in range(size)])


def shards_fn(
    shards,
    spots,
    latents,
    gain_one,
    query_one,
    key_one,
    value_one,
    out_one,
    gain_two,
    query_two,
    key_two,
    value_two,
    out_two,
):
    frames, local, width = latents.shape
    chips = spots // 2
    each = frames // chips
    share = local // shards
    turns = TURNS if share % (8 * TURNS) == 0 else 1
    zf = lax.axis_index("frame")
    chip = lax.axis_index("pos") // 2
    ids = jnp.stack([zf, chip]).astype(jnp.int32)
    row = lambda g: g.reshape(1, -1)

    over_shards = lambda v: [v[0]] + [swap(v[t], "frame", shards, t) for t in range(1, shards)]
    over_chips = lambda v: [v[0]] + [swap(v[s], "pos", spots, 2 * s) for s in range(1, chips)]
    half = max(1, each // SPLIT)
    cut = lambda s, part: lax.dynamic_slice_in_dim(
        latents, (chip ^ s) * each + part * half, each - half if part else half, 0
    )
    early = [jnp.concatenate([cut(s, 0), latents[:1]], axis=0) for s in range(chips)]
    early = over_chips(early)
    late = over_chips([cut(s, 1) for s in range(chips)])
    found = jnp.stack([e[half] for e in early])
    hop = shards // 2
    while hop:
        sent = lax.ppermute(found, "frame", [(i, i + hop) for i in range(0, shards, 2 * hop)])
        found = jnp.where(zf % (2 * hop) == hop, sent, found)
        hop //= 2
    early_other = swap(jnp.stack([e[:half] for e in early]), "pos", spots, 1)
    saved = spatial_early(
        early, early_other, row(gain_one), query_one, key_one, value_one, shards, turns
    )
    late = [jnp.concatenate([l, found[s : s + 1]], axis=0) for s, l in enumerate(late)]
    late_other = swap(jnp.stack(late), "pos", spots, 1)
    mid, rest = spatial_first(
        ids, early, late, late_other, row(gain_one), query_one, key_one, value_one, out_one, saved,
        shards, turns,
    )
    saved = (*saved, *rest)
    step = share // turns
    flat = lambda v: [m.reshape(m.shape[0], each * step, width) for m in v]
    heads = lambda v: [m[0] for m in v]
    across = lambda v, n: [None] + [jnp.stack([m[i] for m in v]) for i in range(1, n)]
    whole = blank(latents.shape)
    weights = (row(gain_two), query_two, key_two, value_two, out_two)
    for turn in range(turns):
        if turn == 0:
            got = over_shards(mid)
            gate = got[1:]
            got = flat(got)
            came = over_chips([None] + across(got, chips)[1:])
        else:
            mid = spatial_later(ids, early, late, saved, out_one, shards, turns, turn)
            mid, _ = lax.optimization_barrier((mid, gate[0]))
            got = flat(over_chips(mid))
            came = over_shards([None] + across(got, shards)[1:])
        if turn:
            came, done = lax.optimization_barrier((came[1:], done))
            came = [None] + list(came)
        done = temporal(heads(got), came[1:], *weights, step, turn == 0)
        back = over_shards(done)
        whole = assemble(ids, [d.reshape(chips, each, step, width) for d in back], whole, turn)
    return whole


def solution(mesh):
    return jax.shard_map(
        functools.partial(shards_fn, mesh.shape["frame"], mesh.shape["pos"]),
        mesh=mesh,
        in_specs=(P("frame", "pos", None), P(), P(), P(), P(), P(), P(), P(), P(), P(), P()),
        out_specs=P("frame", "pos", None),
        check_vma=False,
    )
```

```python
import functools

import jax
import jax.numpy as jnp
from jax import lax
from jax.experimental import pallas as pl
from jax.experimental.pallas import tpu as pltpu
from jax.sharding import PartitionSpec as P

HEADS = 4
LANES = 128
READY = 40
SPLIT = 8
LATER = 6.4
ROOM = 26 * 2**20
TURNS = 2
LOG2E = 1.4426950408889634


def normed(wide, gain):
    factor = lax.rsqrt(jnp.mean(wide * wide, axis=-1, keepdims=True) + 1e-06)
    return wide * factor * gain


def dot(left, right):
    return jnp.dot(left, right, preferred_element_type=jnp.float32)


def dot_t(left, right):
    return lax.dot_general(
        left, right, (((1,), (1,)), ((), ())), preferred_element_type=jnp.float32
    )


def project(pieces, gain_ref, wk_ref, wv_ref, k_ref, v_ref):
    frames, local, width = pieces[0].shape
    gain = gain_ref[...]
    normal = [normed(r.reshape(frames * local, width).astype(jnp.float32), gain) for r in pieces]
    short = [n.astype(jnp.bfloat16) for n in normal]
    for weight, out in ((wk_ref, k_ref), (wv_ref, v_ref)):
        for s, n in enumerate(short):
            got = dot(n, weight[...]).astype(jnp.bfloat16)
            out[:, s * local : (s + 1) * local, :] = got.reshape(frames, local, width)
    return [n.reshape(frames, local, width) for n in normal]


def pick(rows, chips, turns, turn):
    local = rows.shape[0] // chips
    run = local // turns
    return jnp.concatenate(
        [rows[s * local + turn * run : s * local + (turn + 1) * run] for s in range(chips)], axis=0
    )


def attend(turns, turn, zf, pieces, q_ref, k_refs, v_refs, wo_ref, outs, mid_s):
    chips = len(pieces)
    shards, step, width = len(outs), *outs[0].shape[2:]
    half = width // 2
    depth = width // HEADS
    rows = chips * shards * step
    frames = q_ref.shape[0]
    places = 2 * k_refs[0].shape[1]
    low = lax.broadcasted_iota(jnp.int32, (rows, half), 1) < depth
    ones = jnp.ones((2 * places, half), jnp.bfloat16)
    both = lambda refs, f, cols: jnp.concatenate(
        [refs[0][f, :, cols], refs[1][f, :, cols], refs[2][0, :, cols], refs[3][0, :, cols]], axis=0
    )
    together = max(1, min(frames, ROOM // (2 * (2 * rows) * (2 * places) * 6)))
    for start in range(0, frames, together):
        now = range(start, min(start + together, frames))
        items = [(f, slice(p * half, (p + 1) * half)) for f in now for p in range(2)]
        scores = []
        for f, cols in items:
            q = q_ref[f, turn * rows : (turn + 1) * rows, cols]
            zero = jnp.zeros_like(q)
            q = jnp.concatenate([jnp.where(low, q, zero), jnp.where(low, zero, q)], axis=0)
            scores.append(dot_t(q, both(k_refs, f, cols)))
        weights = [
            jnp.exp2(s - jnp.max(s, axis=-1, keepdims=True)).astype(jnp.bfloat16) for s in scores
        ]
        sums = []
        for w, (f, cols) in zip(weights, items):
            r = dot(w, jnp.concatenate([both(v_refs, f, cols), ones], axis=1))
            top = jnp.where(low, r[:rows, :half], r[rows:, :half])
            bottom = jnp.where(low, r[:rows, half:], r[rows:, half:])
            sums.append(top / bottom)
        for u, f in enumerate(now):
            a = jnp.concatenate(sums[2 * u : 2 * u + 2], axis=1).astype(jnp.bfloat16)
            x = jnp.concatenate([r[f].astype(jnp.float32) for r in pieces], axis=0)
            mid_s[f] = pick(x, chips, turns, turn) + dot(a, wo_ref[...])
    for f in range(frames):
        for t in range(shards):
            for s in range(chips):
                at = pl.multiple_of((s * shards + (t ^ zf)) * step, step)
                outs[t][s, f] = mid_s[f, pl.ds(at, step), :].astype(jnp.bfloat16)


def ready_kernel(chips, turns, *refs):
    mine, (gain, wq, wk, wv, q_ref, k_ref, v_ref) = refs[:chips], refs[chips:]
    normal = project([r[...] for r in mine], gain, wk, wv, k_ref, v_ref)
    scale = (wq.shape[0] // HEADS) ** -0.5 * LOG2E
    for f in range(q_ref.shape[0]):
        n = jnp.concatenate([w[f] for w in normal], axis=0)
        n = jnp.concatenate([pick(n, chips, turns, j) for j in range(turns)], axis=0)
        q_ref[f] = (dot(n.astype(jnp.bfloat16), wq[...]) * scale).astype(jnp.bfloat16)


def rest_kernel(chips, other, gain, wk, wv, k_ref, v_ref):
    project([other[s] for s in range(chips)], gain, wk, wv, k_ref, v_ref)


def first_kernel(chips, shards, turns, ids_ref, *refs):
    mine, (near, far, gain, wk, wv, wo, q, k, v, ko, vo) = refs[:chips], refs[chips : chips + 11]
    outs, saved = refs[chips + 11 : chips + 11 + shards], refs[chips + 11 + shards :]
    kn, vn, kf, vf, mid_s = saved
    project([near[s : s + 1] for s in range(chips)], gain, wk, wv, kn, vn)
    project([far[s : s + 1] for s in range(chips)], gain, wk, wv, kf, vf)
    attend(turns, 0, ids_ref[0], mine, q, (k, ko, kn, kf), (v, vo, vn, vf), wo, outs, mid_s)


def later_kernel(chips, turns, turn, ids_ref, *refs):
    mine, (q, k, v, ko, vo, kn, vn, kf, vf, wo) = refs[:chips], refs[chips : chips + 10]
    keys, values, outs = (k, ko, kn, kf), (v, vo, vn, vf), refs[chips + 10 : -1]
    attend(turns, turn, ids_ref[0], mine, q, keys, values, wo, outs, refs[-1])


def vmem(count):
    return [pl.BlockSpec(memory_space=pltpu.VMEM)] * count


def cost(microseconds):
    return pl.CostEstimate(
        flops=int(microseconds * 1e9), bytes_accessed=int(microseconds * 3.6e6), transcendentals=0
    )


def params():
    return pltpu.CompilerParams(vmem_limit_bytes=40 * 2**20)


def shape(*sizes):
    return jax.ShapeDtypeStruct(sizes, jnp.bfloat16)


def spatial_ready(mine, gain, wq, wk, wv, turns):
    chips = len(mine)
    frames, local, width = mine[0].shape
    args = (*mine, gain, wq, wk, wv)
    keys = shape(frames, chips * local, width)
    return pl.pallas_call(
        functools.partial(ready_kernel, chips, turns),
        in_specs=vmem(len(args)),
        out_specs=vmem(3),
        out_shape=[shape(frames, chips * local, width), keys, keys],
        compiler_params=params(),
        cost_estimate=cost(READY),
        name="spatial_ready",
    )(*args)


def spatial_rest(other, gain, wk, wv):
    chips, frames, local, width = other.shape
    args = (other, gain, wk, wv)
    return pl.pallas_call(
        functools.partial(rest_kernel, chips),
        in_specs=vmem(len(args)),
        out_specs=vmem(2),
        out_shape=[shape(frames, chips * local, width)] * 2,
        compiler_params=params(),
        cost_estimate=cost(1),
        name="spatial_rest",
    )(*args)


def spatial_first(ids, mine, near, far, gain, wk, wv, wo, saved, shards, turns):
    chips = len(mine)
    frames, local, width = mine[0].shape
    step = local // shards // turns
    args = (*mine, near, far, gain, wk, wv, wo, *saved)
    out = [shape(chips, frames, step, width)] * shards + [shape(1, chips * local, width)] * 4
    got = pl.pallas_call(
        functools.partial(first_kernel, chips, shards, turns),
        in_specs=[pl.BlockSpec(memory_space=pltpu.SMEM)] + vmem(len(args)),
        out_specs=vmem(len(out)),
        out_shape=out,
        scratch_shapes=[pltpu.VMEM((frames, chips * shards * step, width), jnp.float32)],
        compiler_params=params(),
        cost_estimate=cost(6.5),
        name="spatial_first",
    )(ids, *args)
    return got[:shards], got[shards:]


def spatial_later(ids, mine, saved, wo, shards, turns, turn):
    chips = len(mine)
    frames, local, width = mine[0].shape
    step = local // shards // turns
    args = (*mine, *saved, wo)
    return pl.pallas_call(
        functools.partial(later_kernel, chips, turns, turn),
        in_specs=[pl.BlockSpec(memory_space=pltpu.SMEM)] + vmem(len(args)),
        out_specs=vmem(shards),
        out_shape=[shape(chips, frames, step, width)] * shards,
        scratch_shapes=[pltpu.VMEM((frames, chips * shards * step, width), jnp.float32)],
        compiler_params=params(),
        cost_estimate=cost(LATER),
        name="spatial_later",
    )(ids, *args)


def take(ref, rows):
    return jnp.concatenate([ref[i, rows, :] for i in range(ref.shape[0])], axis=1)


def put(ref, rows, value):
    for i in range(ref.shape[0]):
        ref[i, rows, :] = value[:, i * LANES : (i + 1) * LANES]


def temporal_kernel(chips, shards, share, by_shard, *refs):
    near, far = (shards, chips) if by_shard else (chips, shards)
    own, refs = refs[:near], refs[near:]
    came, refs = refs[: far - 1], refs[far - 1 :]
    gain_ref, wq_ref, wk_ref, wv_ref, wo_ref = refs[:5]
    outs = refs[5 : 5 + shards]
    x_s, q_s, k_s, v_s, a_s = refs[5 + shards :]
    width = wq_ref.shape[0]
    depth = width // HEADS
    half = width // 2
    block = own[0].shape[0]
    frames = block // share * chips * shards
    for t in range(shards):
        for s in range(chips):
            i, j = (t, s) if by_shard else (s, t)
            piece = own[i][...] if j == 0 else came[j - 1][i]
            put(x_s, pl.ds((t * chips + s) * block, block), piece.astype(jnp.float32))
    gain = gain_ref[...]
    for p in range(share):
        n = normed(take(x_s, pl.ds(p, frames, stride=share)), gain).astype(jnp.bfloat16)
        q_s[p] = (dot(n, wq_ref[...]) * (depth**-0.5 * LOG2E)).astype(jnp.bfloat16)
        k_s[p] = dot(n, wk_ref[...]).astype(jnp.bfloat16)
        v_s[p] = dot(n, wv_ref[...]).astype(jnp.bfloat16)
    lane = lax.broadcasted_iota(jnp.int32, (frames, half), 1)
    low, high = lane < depth, lane >= depth
    ones = [c.astype(jnp.float32).astype(jnp.bfloat16) for c in (low, high)]

    zero = jnp.zeros((frames, half), jnp.bfloat16)
    items = [(p, slice(i * half, (i + 1) * half)) for p in range(share) for i in range(2)]
    scores = []
    for p, cols in items:
        k = k_s[p, :, cols]
        k = jnp.concatenate([jnp.where(low, k, zero), jnp.where(high, k, zero)], axis=0)
        scores.append(dot_t(q_s[p, :, cols], k))
    weights = []
    for s in scores:
        tops = [jnp.max(s[:, i * frames : (i + 1) * frames], axis=-1, keepdims=True) for i in range(2)]
        w = [jnp.exp2(s[:, i * frames : (i + 1) * frames] - tops[i]) for i in range(2)]
        weights.append(jnp.concatenate(w, axis=1).astype(jnp.bfloat16))
    parts = []
    for w, (p, cols) in zip(weights, items):
        v = v_s[p, :, cols]
        v = jnp.concatenate(
            [
                jnp.concatenate([jnp.where(low, v, zero), ones[0]], axis=1),
                jnp.concatenate([jnp.where(high, v, zero), ones[1]], axis=1),
            ],
            axis=0,
        )
        r = dot(w, v)
        parts.append(r[:, :half] / r[:, half:])
    for p in range(share):
        a = jnp.concatenate(parts[2 * p : 2 * p + 2], axis=1).astype(jnp.bfloat16)
        rows = pl.ds(p, frames, stride=share)
        put(a_s, rows, take(x_s, rows) + dot(a, wo_ref[...]))
    for t in range(shards):
        for s in range(chips):
            outs[t][s] = take(a_s, pl.ds((t * chips + s) * block, block)).astype(jnp.bfloat16)


def temporal(own, came, gain, wq, wk, wv, wo, share, by_shard):
    shards, chips = len(own), len(came) + 1
    if not by_shard:
        shards, chips = chips, shards
    block, width = own[0].shape
    rows = block * chips * shards
    frames = rows // share
    return pl.pallas_call(
        functools.partial(temporal_kernel, chips, shards, share, by_shard),
        out_shape=[jax.ShapeDtypeStruct((chips, block, width), jnp.bfloat16)] * shards,
        scratch_shapes=[
            pltpu.VMEM((width // LANES, rows, LANES), jnp.float32),
            pltpu.VMEM((share, frames, width), jnp.bfloat16),
            pltpu.VMEM((share, frames, width), jnp.bfloat16),
            pltpu.VMEM((share, frames, width), jnp.bfloat16),
            pltpu.VMEM((width // LANES, rows, LANES), jnp.float32),
        ],
        compiler_params=pltpu.CompilerParams(vmem_limit_bytes=48 * 2**20),
        cost_estimate=cost(1.9),
        name="temporal",
    )(*own, *came, gain, wq, wk, wv, wo)


def assemble_kernel(turn, ids_ref, *refs):
    shards = len(refs) - 4
    pieces, (_, out_ref, held, sem) = refs[:shards], refs[shards:]
    chips, frames, step, _ = pieces[0].shape
    run = shards * step
    for z in range(shards):

        @pl.when(ids_ref[0] == z)
        def _():
            for s in range(chips):
                got = [pieces[g ^ z][s].astype(jnp.float32) for g in range(shards)]
                held[pl.ds((s ^ ids_ref[1]) * frames, frames)] = jnp.concatenate(got, axis=1).astype(
                    jnp.bfloat16
                )

    copy = pltpu.make_async_copy(held, out_ref.at[:, pl.ds(turn * run, run), :], sem)
    copy.start()
    copy.wait()


def assemble(ids, pieces, whole, turn):
    shards = len(pieces)
    chips, frames, step, width = pieces[0].shape
    return pl.pallas_call(
        functools.partial(assemble_kernel, turn),
        in_specs=[pl.BlockSpec(memory_space=pltpu.SMEM)]
        + vmem(shards)
        + [pl.BlockSpec(memory_space=pl.ANY)],
        out_specs=pl.BlockSpec(memory_space=pl.ANY),
        out_shape=jax.ShapeDtypeStruct(whole.shape, whole.dtype),
        scratch_shapes=[
            pltpu.VMEM((chips * frames, shards * step, width), jnp.bfloat16),
            pltpu.SemaphoreType.DMA(()),
        ],
        input_output_aliases={shards + 1: 0},
        compiler_params=params(),
        cost_estimate=cost(60 if turn == 0 else 1),
        name="assemble",
    )(ids, *pieces, whole)


def blank(sizes):
    return pl.pallas_call(
        lambda out_ref: None,
        out_specs=pl.BlockSpec(memory_space=pl.ANY),
        out_shape=shape(*sizes),
        name="blank",
    )()


def swap(value, axis, size, mask):
    return lax.ppermute(value, axis, [(i, i ^ mask) for i in range(size)])


def shards_fn(
    shards,
    spots,
    latents,
    gain_one,
    query_one,
    key_one,
    value_one,
    out_one,
    gain_two,
    query_two,
    key_two,
    value_two,
    out_two,
):
    frames, local, width = latents.shape
    chips = spots // 2
    each = frames // chips
    share = local // shards
    turns = TURNS if share % (8 * TURNS) == 0 else 1
    zf = lax.axis_index("frame")
    chip = lax.axis_index("pos") // 2
    ids = jnp.stack([zf, chip]).astype(jnp.int32)
    row = lambda g: g.reshape(1, -1)

    over_shards = lambda v: [v[0]] + [swap(v[t], "frame", shards, t) for t in range(1, shards)]
    over_chips = lambda v: [v[0]] + [swap(v[s], "pos", spots, 2 * s) for s in range(1, chips)]
    half = max(1, each // SPLIT)
    cut = lambda s, part: lax.dynamic_slice_in_dim(
        latents, (chip ^ s) * each + part * half, each - half if part else half, 0
    )
    early = [jnp.concatenate([cut(s, 0), latents[:1]], axis=0) for s in range(chips)]
    early = over_chips(early)
    late = over_chips([cut(s, 1) for s in range(chips)])
    found = jnp.stack([e[half] for e in early])
    hop = shards // 2
    while hop:
        sent = lax.ppermute(found, "frame", [(i, i + hop) for i in range(0, shards, 2 * hop)])
        found = jnp.where(zf % (2 * hop) == hop, sent, found)
        hop //= 2
    mine = [jnp.concatenate([e[:half], l], axis=0) for e, l in zip(early, late)]
    saved = spatial_ready(mine, row(gain_one), query_one, key_one, value_one, turns)
    rest = spatial_rest(
        swap(jnp.stack(mine), "pos", spots, 1), row(gain_one), key_one, value_one
    )
    saved = (*saved, *rest)
    far = swap(found, "pos", spots, 1)
    mid, ends = spatial_first(
        ids, mine, found, far, row(gain_one), key_one, value_one, out_one, saved, shards, turns
    )
    saved = (*saved, *ends)
    step = share // turns
    flat = lambda v: [m.reshape(m.shape[0], each * step, width) for m in v]
    heads = lambda v: [m[0] for m in v]
    across = lambda v, n: [None] + [jnp.stack([m[i] for m in v]) for i in range(1, n)]
    whole = blank(latents.shape)
    weights = (row(gain_two), query_two, key_two, value_two, out_two)
    mids = [mid]
    for turn in range(1, turns):
        mids.append(spatial_later(ids, mine, saved, out_one, shards, turns, turn))
    pass
    got = [over_shards(mid) for mid in mids]
    done = None
    for turn in range(turns):
        now = got[turn]
        if turn + 1 < turns:
            more = got[turn + 1]
            now, mids[1] = lax.optimization_barrier((now, mids[1]))
        if turn:
            now, _ = lax.optimization_barrier((now, done))
        came = over_chips([None] + across(flat(now), chips)[1:])[1:]
        if turn + 1 < turns:
            came, _ = lax.optimization_barrier((came, more[1:3]))
        if turn:
            came, done = lax.optimization_barrier((came, done))
        done = temporal(heads(flat(now)), came, *weights, step, True)
        back = over_shards(done)
        whole = assemble(ids, [d.reshape(chips, each, step, width) for d in back], whole, turn)
    return whole


def solution(mesh):
    return jax.shard_map(
        functools.partial(shards_fn, mesh.shape["frame"], mesh.shape["pos"]),
        mesh=mesh,
        in_specs=(P("frame", "pos", None), P(), P(), P(), P(), P(), P(), P(), P(), P(), P()),
        out_specs=P("frame", "pos", None),
        check_vma=False,
    )
```

```python
import functools

import jax
import jax.numpy as jnp
from jax import lax
from jax.experimental import pallas as pl
from jax.experimental.pallas import tpu as pltpu
from jax.sharding import PartitionSpec as P

HEADS = 4
LANES = 128
READY = 40
SPLIT = 8
LATER = 6.4
ROOM = 26 * 2**20
TURNS = 2
LOG2E = 1.4426950408889634


def normed(wide, gain):
    factor = lax.rsqrt(jnp.mean(wide * wide, axis=-1, keepdims=True) + 1e-06)
    return wide * factor * gain


def dot(left, right):
    return jnp.dot(left, right, preferred_element_type=jnp.float32)


def dot_t(left, right):
    return lax.dot_general(
        left, right, (((1,), (1,)), ((), ())), preferred_element_type=jnp.float32
    )


def project(pieces, gain_ref, wk_ref, wv_ref, k_ref, v_ref):
    frames, local, width = pieces[0].shape
    gain = gain_ref[...]
    normal = [normed(r.reshape(frames * local, width).astype(jnp.float32), gain) for r in pieces]
    short = [n.astype(jnp.bfloat16) for n in normal]
    for weight, out in ((wk_ref, k_ref), (wv_ref, v_ref)):
        for s, n in enumerate(short):
            got = dot(n, weight[...]).astype(jnp.bfloat16)
            out[:, s * local : (s + 1) * local, :] = got.reshape(frames, local, width)
    return [n.reshape(frames, local, width) for n in normal]


def mask(place, shards):
    return (shards - place) % shards


def pick(rows, chips, turns, turn):
    local = rows.shape[0] // chips
    run = local // turns
    return jnp.concatenate(
        [rows[s * local + turn * run : s * local + (turn + 1) * run] for s in range(chips)], axis=0
    )


def attend(turns, turn, zf, pieces, q_ref, k_refs, v_refs, wo_ref, outs, mid_s):
    chips = len(pieces)
    shards, step, width = len(outs), *outs[0].shape[2:]
    half = width // 2
    depth = width // HEADS
    rows = chips * shards * step
    frames = q_ref.shape[0]
    places = 2 * k_refs[0].shape[1]
    low = lax.broadcasted_iota(jnp.int32, (rows, half), 1) < depth
    ones = jnp.ones((2 * places, half), jnp.bfloat16)
    both = lambda refs, f, cols: jnp.concatenate(
        [refs[0][f, :, cols], refs[1][f, :, cols], refs[2][0, :, cols], refs[3][0, :, cols]], axis=0
    )
    together = max(1, min(frames, ROOM // (2 * (2 * rows) * (2 * places) * 6)))
    for start in range(0, frames, together):
        now = range(start, min(start + together, frames))
        items = [(f, slice(p * half, (p + 1) * half)) for f in now for p in range(2)]
        scores = []
        for f, cols in items:
            q = q_ref[f, turn * rows : (turn + 1) * rows, cols]
            zero = jnp.zeros_like(q)
            q = jnp.concatenate([jnp.where(low, q, zero), jnp.where(low, zero, q)], axis=0)
            scores.append(dot_t(q, both(k_refs, f, cols)))
        weights = [
            jnp.exp2(s - jnp.max(s, axis=-1, keepdims=True)).astype(jnp.bfloat16) for s in scores
        ]
        sums = []
        for w, (f, cols) in zip(weights, items):
            r = dot(w, jnp.concatenate([both(v_refs, f, cols), ones], axis=1))
            top = jnp.where(low, r[:rows, :half], r[rows:, :half])
            bottom = jnp.where(low, r[:rows, half:], r[rows:, half:])
            sums.append(top / bottom)
        for u, f in enumerate(now):
            a = jnp.concatenate(sums[2 * u : 2 * u + 2], axis=1).astype(jnp.bfloat16)
            x = jnp.concatenate([r[f].astype(jnp.float32) for r in pieces], axis=0)
            mid_s[f] = pick(x, chips, turns, turn) + dot(a, wo_ref[...])
    for f in range(frames):
        for t in range(shards):
            for s in range(chips):
                at = pl.multiple_of((s * shards + (mask(t, shards) ^ zf)) * step, step)
                outs[t][s, f] = mid_s[f, pl.ds(at, step), :].astype(jnp.bfloat16)


def ready_kernel(chips, turns, *refs):
    mine, (gain, wq, wk, wv, q_ref, k_ref, v_ref) = refs[:chips], refs[chips:]
    normal = project([r[...] for r in mine], gain, wk, wv, k_ref, v_ref)
    scale = (wq.shape[0] // HEADS) ** -0.5 * LOG2E
    for f in range(q_ref.shape[0]):
        n = jnp.concatenate([w[f] for w in normal], axis=0)
        n = jnp.concatenate([pick(n, chips, turns, j) for j in range(turns)], axis=0)
        q_ref[f] = (dot(n.astype(jnp.bfloat16), wq[...]) * scale).astype(jnp.bfloat16)


def rest_kernel(chips, other, gain, wk, wv, k_ref, v_ref):
    project([other[s] for s in range(chips)], gain, wk, wv, k_ref, v_ref)


def first_kernel(chips, shards, turns, ids_ref, *refs):
    mine, (near, far, gain, wk, wv, wo, q, k, v, ko, vo) = refs[:chips], refs[chips : chips + 11]
    outs, saved = refs[chips + 11 : chips + 11 + shards], refs[chips + 11 + shards :]
    kn, vn, kf, vf, mid_s = saved
    project([near[s : s + 1] for s in range(chips)], gain, wk, wv, kn, vn)
    project([far[s : s + 1] for s in range(chips)], gain, wk, wv, kf, vf)
    attend(turns, 0, ids_ref[0], mine, q, (k, ko, kn, kf), (v, vo, vn, vf), wo, outs, mid_s)


def later_kernel(chips, turns, turn, ids_ref, *refs):
    mine, (q, k, v, ko, vo, kn, vn, kf, vf, wo) = refs[:chips], refs[chips : chips + 10]
    keys, values, outs = (k, ko, kn, kf), (v, vo, vn, vf), refs[chips + 10 : -1]
    attend(turns, turn, ids_ref[0], mine, q, keys, values, wo, outs, refs[-1])


def vmem(count):
    return [pl.BlockSpec(memory_space=pltpu.VMEM)] * count


def cost(microseconds):
    return pl.CostEstimate(
        flops=int(microseconds * 1e9), bytes_accessed=int(microseconds * 3.6e6), transcendentals=0
    )


def params():
    return pltpu.CompilerParams(vmem_limit_bytes=40 * 2**20)


def shape(*sizes):
    return jax.ShapeDtypeStruct(sizes, jnp.bfloat16)


def spatial_ready(mine, gain, wq, wk, wv, turns):
    chips = len(mine)
    frames, local, width = mine[0].shape
    args = (*mine, gain, wq, wk, wv)
    keys = shape(frames, chips * local, width)
    return pl.pallas_call(
        functools.partial(ready_kernel, chips, turns),
        in_specs=vmem(len(args)),
        out_specs=vmem(3),
        out_shape=[shape(frames, chips * local, width), keys, keys],
        compiler_params=params(),
        cost_estimate=cost(READY),
        name="spatial_ready",
    )(*args)


def spatial_rest(other, gain, wk, wv):
    chips, frames, local, width = other.shape
    args = (other, gain, wk, wv)
    return pl.pallas_call(
        functools.partial(rest_kernel, chips),
        in_specs=vmem(len(args)),
        out_specs=vmem(2),
        out_shape=[shape(frames, chips * local, width)] * 2,
        compiler_params=params(),
        cost_estimate=cost(40),
        name="spatial_rest",
    )(*args)


def spatial_first(ids, mine, near, far, gain, wk, wv, wo, saved, shards, turns):
    chips = len(mine)
    frames, local, width = mine[0].shape
    step = local // shards // turns
    args = (*mine, near, far, gain, wk, wv, wo, *saved)
    out = [shape(chips, frames, step, width)] * shards + [shape(1, chips * local, width)] * 4
    got = pl.pallas_call(
        functools.partial(first_kernel, chips, shards, turns),
        in_specs=[pl.BlockSpec(memory_space=pltpu.SMEM)] + vmem(len(args)),
        out_specs=vmem(len(out)),
        out_shape=out,
        scratch_shapes=[pltpu.VMEM((frames, chips * shards * step, width), jnp.float32)],
        compiler_params=params(),
        cost_estimate=cost(6.5),
        name="spatial_first",
    )(ids, *args)
    return got[:shards], got[shards:]


def spatial_later(ids, mine, saved, wo, shards, turns, turn):
    chips = len(mine)
    frames, local, width = mine[0].shape
    step = local // shards // turns
    args = (*mine, *saved, wo)
    return pl.pallas_call(
        functools.partial(later_kernel, chips, turns, turn),
        in_specs=[pl.BlockSpec(memory_space=pltpu.SMEM)] + vmem(len(args)),
        out_specs=vmem(shards),
        out_shape=[shape(chips, frames, step, width)] * shards,
        scratch_shapes=[pltpu.VMEM((frames, chips * shards * step, width), jnp.float32)],
        compiler_params=params(),
        cost_estimate=cost(LATER),
        name="spatial_later",
    )(ids, *args)


def take(ref, rows):
    return jnp.concatenate([ref[i, rows, :] for i in range(ref.shape[0])], axis=1)


def put(ref, rows, value):
    for i in range(ref.shape[0]):
        ref[i, rows, :] = value[:, i * LANES : (i + 1) * LANES]


def temporal_kernel(chips, shards, share, by_shard, *refs):
    near, far = (shards, chips) if by_shard else (chips, shards)
    own, refs = refs[:near], refs[near:]
    came, refs = refs[: far - 1], refs[far - 1 :]
    gain_ref, wq_ref, wk_ref, wv_ref, wo_ref = refs[:5]
    outs = refs[5 : 5 + shards]
    x_s, q_s, k_s, v_s, a_s = refs[5 + shards :]
    width = wq_ref.shape[0]
    depth = width // HEADS
    half = width // 2
    block = own[0].shape[0]
    frames = block // share * chips * shards
    for t in range(shards):
        for s in range(chips):
            i, j = (t, s) if by_shard else (s, t)
            piece = own[i][...] if j == 0 else came[j - 1][i]
            put(x_s, pl.ds((t * chips + s) * block, block), piece.astype(jnp.float32))
    gain = gain_ref[...]
    for p in range(share):
        n = normed(take(x_s, pl.ds(p, frames, stride=share)), gain).astype(jnp.bfloat16)
        q_s[p] = (dot(n, wq_ref[...]) * (depth**-0.5 * LOG2E)).astype(jnp.bfloat16)
        k_s[p] = dot(n, wk_ref[...]).astype(jnp.bfloat16)
        v_s[p] = dot(n, wv_ref[...]).astype(jnp.bfloat16)
    lane = lax.broadcasted_iota(jnp.int32, (frames, half), 1)
    low, high = lane < depth, lane >= depth
    ones = [c.astype(jnp.float32).astype(jnp.bfloat16) for c in (low, high)]

    zero = jnp.zeros((frames, half), jnp.bfloat16)
    items = [(p, slice(i * half, (i + 1) * half)) for p in range(share) for i in range(2)]
    scores = []
    for p, cols in items:
        k = k_s[p, :, cols]
        k = jnp.concatenate([jnp.where(low, k, zero), jnp.where(high, k, zero)], axis=0)
        scores.append(dot_t(q_s[p, :, cols], k))
    weights = []
    for s in scores:
        tops = [jnp.max(s[:, i * frames : (i + 1) * frames], axis=-1, keepdims=True) for i in range(2)]
        w = [jnp.exp2(s[:, i * frames : (i + 1) * frames] - tops[i]) for i in range(2)]
        weights.append(jnp.concatenate(w, axis=1).astype(jnp.bfloat16))
    parts = []
    for w, (p, cols) in zip(weights, items):
        v = v_s[p, :, cols]
        v = jnp.concatenate(
            [
                jnp.concatenate([jnp.where(low, v, zero), ones[0]], axis=1),
                jnp.concatenate([jnp.where(high, v, zero), ones[1]], axis=1),
            ],
            axis=0,
        )
        r = dot(w, v)
        parts.append(r[:, :half] / r[:, half:])
    for p in range(share):
        a = jnp.concatenate(parts[2 * p : 2 * p + 2], axis=1).astype(jnp.bfloat16)
        rows = pl.ds(p, frames, stride=share)
        put(a_s, rows, take(x_s, rows) + dot(a, wo_ref[...]))
    for t in range(shards):
        for s in range(chips):
            outs[t][s] = take(a_s, pl.ds((t * chips + s) * block, block)).astype(jnp.bfloat16)


def temporal(own, came, gain, wq, wk, wv, wo, share, by_shard):
    shards, chips = len(own), len(came) + 1
    if not by_shard:
        shards, chips = chips, shards
    block, width = own[0].shape
    rows = block * chips * shards
    frames = rows // share
    return pl.pallas_call(
        functools.partial(temporal_kernel, chips, shards, share, by_shard),
        out_shape=[jax.ShapeDtypeStruct((chips, block, width), jnp.bfloat16)] * shards,
        scratch_shapes=[
            pltpu.VMEM((width // LANES, rows, LANES), jnp.float32),
            pltpu.VMEM((share, frames, width), jnp.bfloat16),
            pltpu.VMEM((share, frames, width), jnp.bfloat16),
            pltpu.VMEM((share, frames, width), jnp.bfloat16),
            pltpu.VMEM((width // LANES, rows, LANES), jnp.float32),
        ],
        compiler_params=pltpu.CompilerParams(vmem_limit_bytes=48 * 2**20),
        cost_estimate=cost(1.9),
        name="temporal",
    )(*own, *came, gain, wq, wk, wv, wo)


def assemble_kernel(turn, ids_ref, *refs):
    shards = len(refs) - 4
    pieces, (_, out_ref, held, sem) = refs[:shards], refs[shards:]
    chips, frames, step, _ = pieces[0].shape
    run = shards * step
    for z in range(shards):

        @pl.when(ids_ref[0] == z)
        def _():
            for s in range(chips):
                got = [pieces[mask(g ^ z, shards)][s].astype(jnp.float32) for g in range(shards)]
                held[pl.ds((s ^ ids_ref[1]) * frames, frames)] = jnp.concatenate(got, axis=1).astype(
                    jnp.bfloat16
                )

    copy = pltpu.make_async_copy(held, out_ref.at[:, pl.ds(turn * run, run), :], sem)
    copy.start()
    copy.wait()


def assemble(ids, pieces, whole, turn):
    shards = len(pieces)
    chips, frames, step, width = pieces[0].shape
    return pl.pallas_call(
        functools.partial(assemble_kernel, turn),
        in_specs=[pl.BlockSpec(memory_space=pltpu.SMEM)]
        + vmem(shards)
        + [pl.BlockSpec(memory_space=pl.ANY)],
        out_specs=pl.BlockSpec(memory_space=pl.ANY),
        out_shape=jax.ShapeDtypeStruct(whole.shape, whole.dtype),
        scratch_shapes=[
            pltpu.VMEM((chips * frames, shards * step, width), jnp.bfloat16),
            pltpu.SemaphoreType.DMA(()),
        ],
        input_output_aliases={shards + 1: 0},
        compiler_params=params(),
        cost_estimate=cost(60 if turn == 0 else 1),
        name="assemble",
    )(ids, *pieces, whole)


def blank(sizes):
    return pl.pallas_call(
        lambda out_ref: None,
        out_specs=pl.BlockSpec(memory_space=pl.ANY),
        out_shape=shape(*sizes),
        name="blank",
    )()


def swap(value, axis, size, mask):
    return lax.ppermute(value, axis, [(i, i ^ mask) for i in range(size)])


def shards_fn(
    shards,
    spots,
    latents,
    gain_one,
    query_one,
    key_one,
    value_one,
    out_one,
    gain_two,
    query_two,
    key_two,
    value_two,
    out_two,
):
    frames, local, width = latents.shape
    chips = spots // 2
    each = frames // chips
    share = local // shards
    turns = TURNS if share % (8 * TURNS) == 0 else 1
    zf = lax.axis_index("frame")
    chip = lax.axis_index("pos") // 2
    ids = jnp.stack([zf, chip]).astype(jnp.int32)
    row = lambda g: g.reshape(1, -1)

    over_shards = lambda v: [v[0]] + [swap(v[t], "frame", shards, mask(t, shards)) for t in range(1, shards)]
    over_chips = lambda v: [v[0]] + [swap(v[s], "pos", spots, 2 * s) for s in range(1, chips)]
    half = max(1, each // SPLIT)
    cut = lambda s, part: lax.dynamic_slice_in_dim(
        latents, (chip ^ s) * each + part * half, each - half if part else half, 0
    )
    early = [jnp.concatenate([cut(s, 0), latents[:1]], axis=0) for s in range(chips)]
    early = over_chips(early)
    late = over_chips([cut(s, 1) for s in range(chips)])
    found = jnp.stack([e[half] for e in early])
    hop = shards // 2
    while hop:
        sent = lax.ppermute(found, "frame", [(i, i + hop) for i in range(0, shards, 2 * hop)])
        found = jnp.where(zf % (2 * hop) == hop, sent, found)
        hop //= 2
    mine = [jnp.concatenate([e[:half], l], axis=0) for e, l in zip(early, late)]
    saved = spatial_ready(mine, row(gain_one), query_one, key_one, value_one, turns)
    rest = spatial_rest(
        swap(jnp.stack(mine), "pos", spots, 1), row(gain_one), key_one, value_one
    )
    found, ready = lax.optimization_barrier((found, saved))
    saved = (*saved, *rest)
    far = swap(found, "pos", spots, 1)
    mid, ends = spatial_first(
        ids, mine, found, far, row(gain_one), key_one, value_one, out_one, saved, shards, turns
    )
    saved = (*saved, *ends)
    step = share // turns
    flat = lambda v: [m.reshape(m.shape[0], each * step, width) for m in v]
    heads = lambda v: [m[0] for m in v]
    across = lambda v, n: [None] + [jnp.stack([m[i] for m in v]) for i in range(1, n)]
    whole = blank(latents.shape)
    weights = (row(gain_two), query_two, key_two, value_two, out_two)
    mids = [mid]
    for turn in range(1, turns):
        mids.append(spatial_later(ids, mine, saved, out_one, shards, turns, turn))
    pass
    got = [over_shards(mid) for mid in mids]
    done = None
    for turn in range(turns):
        now = got[turn]
        if turn + 1 < turns:
            more = got[turn + 1]
            now, mids[1] = lax.optimization_barrier((now, mids[1]))
        if turn:
            now, _ = lax.optimization_barrier((now, done))
        came = over_chips([None] + across(flat(now), chips)[1:])[1:]
        if turn + 1 < turns:
            came, _ = lax.optimization_barrier((came, more[1::2]))
        if turn:
            came, done = lax.optimization_barrier((came, done))
        done = temporal(heads(flat(now)), came, *weights, step, True)
        back = over_shards(done)
        whole = assemble(ids, [d.reshape(chips, each, step, width) for d in back], whole, turn)
    return whole


def solution(mesh):
    return jax.shard_map(
        functools.partial(shards_fn, mesh.shape["frame"], mesh.shape["pos"]),
        mesh=mesh,
        in_specs=(P("frame", "pos", None), P(), P(), P(), P(), P(), P(), P(), P(), P(), P()),
        out_specs=P("frame", "pos", None),
        check_vma=False,
    )
```

```python
import functools

import jax
import jax.numpy as jnp
from jax import lax
from jax.experimental import pallas as pl
from jax.experimental.pallas import tpu as pltpu
from jax.sharding import PartitionSpec as P

HEADS = 4
LANES = 128
READY = 40
SPLIT = 8
LATER = 6.4
ROOM = 26 * 2**20
TURNS = 2
LOG2E = 1.4426950408889634


def normed(wide, gain):
    factor = lax.rsqrt(jnp.mean(wide * wide, axis=-1, keepdims=True) + 1e-06)
    return wide * factor * gain


def dot(left, right):
    return jnp.dot(left, right, preferred_element_type=jnp.float32)


def dot_t(left, right):
    return lax.dot_general(
        left, right, (((1,), (1,)), ((), ())), preferred_element_type=jnp.float32
    )


def project(pieces, gain_ref, wk_ref, wv_ref, k_ref, v_ref):
    frames, local, width = pieces[0].shape
    gain = gain_ref[...]
    normal = [normed(r.reshape(frames * local, width).astype(jnp.float32), gain) for r in pieces]
    short = [n.astype(jnp.bfloat16) for n in normal]
    for weight, out in ((wk_ref, k_ref), (wv_ref, v_ref)):
        for s, n in enumerate(short):
            got = dot(n, weight[...]).astype(jnp.bfloat16)
            out[:, s * local : (s + 1) * local, :] = got.reshape(frames, local, width)
    return [n.reshape(frames, local, width) for n in normal]


def mask(place, shards):
    return (shards - place) % shards


def pick(rows, chips, turns, turn):
    local = rows.shape[0] // chips
    run = local // turns
    return jnp.concatenate(
        [rows[s * local + turn * run : s * local + (turn + 1) * run] for s in range(chips)], axis=0
    )


def attend(turns, turn, zf, pieces, q_ref, k_refs, v_refs, wo_ref, outs, mid_s):
    chips = len(pieces)
    shards, step, width = len(outs), *outs[0].shape[2:]
    half = width // 2
    depth = width // HEADS
    rows = chips * shards * step
    frames = q_ref.shape[0]
    places = 2 * k_refs[0].shape[1]
    low = lax.broadcasted_iota(jnp.int32, (rows, half), 1) < depth
    ones = jnp.ones((2 * places, half), jnp.bfloat16)
    both = lambda refs, f, cols: jnp.concatenate(
        [refs[0][f, :, cols], refs[1][f, :, cols], refs[2][0, :, cols], refs[3][0, :, cols]], axis=0
    )
    together = max(1, min(frames, ROOM // (2 * (2 * rows) * (2 * places) * 6)))
    for start in range(0, frames, together):
        now = range(start, min(start + together, frames))
        items = [(f, slice(p * half, (p + 1) * half)) for f in now for p in range(2)]
        scores = []
        for f, cols in items:
            q = q_ref[f, turn * rows : (turn + 1) * rows, cols]
            zero = jnp.zeros_like(q)
            q = jnp.concatenate([jnp.where(low, q, zero), jnp.where(low, zero, q)], axis=0)
            scores.append(dot_t(q, both(k_refs, f, cols)))
        weights = [
            jnp.exp2(s - jnp.max(s, axis=-1, keepdims=True)).astype(jnp.bfloat16) for s in scores
        ]
        sums = []
        for w, (f, cols) in zip(weights, items):
            r = dot(w, jnp.concatenate([both(v_refs, f, cols), ones], axis=1))
            top = jnp.where(low, r[:rows, :half], r[rows:, :half])
            bottom = jnp.where(low, r[:rows, half:], r[rows:, half:])
            sums.append(top / bottom)
        for u, f in enumerate(now):
            a = jnp.concatenate(sums[2 * u : 2 * u + 2], axis=1).astype(jnp.bfloat16)
            x = jnp.concatenate([r[f].astype(jnp.float32) for r in pieces], axis=0)
            mid_s[f] = pick(x, chips, turns, turn) + dot(a, wo_ref[...])
    for f in range(frames):
        for t in range(shards):
            for s in range(chips):
                at = pl.multiple_of((s * shards + (mask(t, shards) ^ zf)) * step, step)
                outs[t][s, f] = mid_s[f, pl.ds(at, step), :].astype(jnp.bfloat16)


def ready_kernel(chips, turns, *refs):
    mine, (gain, wq, wk, wv, q_ref, k_ref, v_ref) = refs[:chips], refs[chips:]
    normal = project([r[...] for r in mine], gain, wk, wv, k_ref, v_ref)
    scale = (wq.shape[0] // HEADS) ** -0.5 * LOG2E
    for f in range(q_ref.shape[0]):
        n = jnp.concatenate([w[f] for w in normal], axis=0)
        n = jnp.concatenate([pick(n, chips, turns, j) for j in range(turns)], axis=0)
        q_ref[f] = (dot(n.astype(jnp.bfloat16), wq[...]) * scale).astype(jnp.bfloat16)


def rest_kernel(chips, other, gain, wk, wv, k_ref, v_ref):
    project([other[s] for s in range(chips)], gain, wk, wv, k_ref, v_ref)


def first_kernel(chips, shards, turns, ids_ref, *refs):
    mine, (near, far, gain, wk, wv, wo, q, k, v, ko, vo) = refs[:chips], refs[chips : chips + 11]
    outs, saved = refs[chips + 11 : chips + 11 + shards], refs[chips + 11 + shards :]
    kn, vn, kf, vf, mid_s = saved
    project([near[s : s + 1] for s in range(chips)], gain, wk, wv, kn, vn)
    project([far[s : s + 1] for s in range(chips)], gain, wk, wv, kf, vf)
    attend(turns, 0, ids_ref[0], mine, q, (k, ko, kn, kf), (v, vo, vn, vf), wo, outs, mid_s)


def later_kernel(chips, turns, turn, ids_ref, *refs):
    mine, (q, k, v, ko, vo, kn, vn, kf, vf, wo) = refs[:chips], refs[chips : chips + 10]
    keys, values, outs = (k, ko, kn, kf), (v, vo, vn, vf), refs[chips + 10 : -1]
    attend(turns, turn, ids_ref[0], mine, q, keys, values, wo, outs, refs[-1])


def vmem(count):
    return [pl.BlockSpec(memory_space=pltpu.VMEM)] * count


def cost(microseconds):
    return pl.CostEstimate(
        flops=int(microseconds * 1e9), bytes_accessed=int(microseconds * 3.6e6), transcendentals=0
    )


def params():
    return pltpu.CompilerParams(vmem_limit_bytes=40 * 2**20)


def shape(*sizes):
    return jax.ShapeDtypeStruct(sizes, jnp.bfloat16)


def spatial_ready(mine, gain, wq, wk, wv, turns):
    chips = len(mine)
    frames, local, width = mine[0].shape
    args = (*mine, gain, wq, wk, wv)
    keys = shape(frames, chips * local, width)
    return pl.pallas_call(
        functools.partial(ready_kernel, chips, turns),
        in_specs=vmem(len(args)),
        out_specs=vmem(3),
        out_shape=[shape(frames, chips * local, width), keys, keys],
        compiler_params=params(),
        cost_estimate=cost(READY),
        name="spatial_ready",
    )(*args)


def spatial_rest(other, gain, wk, wv):
    chips, frames, local, width = other.shape
    args = (other, gain, wk, wv)
    return pl.pallas_call(
        functools.partial(rest_kernel, chips),
        in_specs=vmem(len(args)),
        out_specs=vmem(2),
        out_shape=[shape(frames, chips * local, width)] * 2,
        compiler_params=params(),
        cost_estimate=cost(40),
        name="spatial_rest",
    )(*args)


def spatial_first(ids, mine, near, far, gain, wk, wv, wo, saved, shards, turns):
    chips = len(mine)
    frames, local, width = mine[0].shape
    step = local // shards // turns
    args = (*mine, near, far, gain, wk, wv, wo, *saved)
    out = [shape(chips, frames, step, width)] * shards + [shape(1, chips * local, width)] * 4
    got = pl.pallas_call(
        functools.partial(first_kernel, chips, shards, turns),
        in_specs=[pl.BlockSpec(memory_space=pltpu.SMEM)] + vmem(len(args)),
        out_specs=vmem(len(out)),
        out_shape=out,
        scratch_shapes=[pltpu.VMEM((frames, chips * shards * step, width), jnp.float32)],
        compiler_params=params(),
        cost_estimate=cost(6.5),
        name="spatial_first",
    )(ids, *args)
    return got[:shards], got[shards:]


def spatial_later(ids, mine, saved, wo, shards, turns, turn):
    chips = len(mine)
    frames, local, width = mine[0].shape
    step = local // shards // turns
    args = (*mine, *saved, wo)
    return pl.pallas_call(
        functools.partial(later_kernel, chips, turns, turn),
        in_specs=[pl.BlockSpec(memory_space=pltpu.SMEM)] + vmem(len(args)),
        out_specs=vmem(shards),
        out_shape=[shape(chips, frames, step, width)] * shards,
        scratch_shapes=[pltpu.VMEM((frames, chips * shards * step, width), jnp.float32)],
        compiler_params=params(),
        cost_estimate=cost(LATER),
        name="spatial_later",
    )(ids, *args)


def take(ref, rows):
    return jnp.concatenate([ref[i, rows, :] for i in range(ref.shape[0])], axis=1)


def put(ref, rows, value):
    for i in range(ref.shape[0]):
        ref[i, rows, :] = value[:, i * LANES : (i + 1) * LANES]


def temporal_kernel(chips, shards, share, by_shard, *refs):
    near, far = (shards, chips) if by_shard else (chips, shards)
    own, refs = refs[:near], refs[near:]
    came, refs = refs[: far - 1], refs[far - 1 :]
    gain_ref, wq_ref, wk_ref, wv_ref, wo_ref = refs[:5]
    outs = refs[5 : 5 + shards]
    x_s, q_s, k_s, v_s, a_s = refs[5 + shards :]
    width = wq_ref.shape[0]
    depth = width // HEADS
    half = width // 2
    block = own[0].shape[0]
    frames = block // share * chips * shards
    for t in range(shards):
        for s in range(chips):
            i, j = (t, s) if by_shard else (s, t)
            piece = own[i][...] if j == 0 else came[j - 1][i]
            put(x_s, pl.ds((t * chips + s) * block, block), piece.astype(jnp.float32))
    gain = gain_ref[...]
    n = [normed(take(x_s, pl.ds(p, frames, stride=share)), gain) for p in range(share)]
    n = jnp.concatenate([v.astype(jnp.bfloat16) for v in n], axis=0)
    q_s[...] = (dot(n, wq_ref[...]) * (depth**-0.5 * LOG2E)).astype(jnp.bfloat16).reshape(q_s.shape)
    k_s[...] = dot(n, wk_ref[...]).astype(jnp.bfloat16).reshape(k_s.shape)
    v_s[...] = dot(n, wv_ref[...]).astype(jnp.bfloat16).reshape(v_s.shape)
    lane = lax.broadcasted_iota(jnp.int32, (frames, half), 1)
    low, high = lane < depth, lane >= depth
    ones = [c.astype(jnp.float32).astype(jnp.bfloat16) for c in (low, high)]

    zero = jnp.zeros((frames, half), jnp.bfloat16)
    items = [(p, slice(i * half, (i + 1) * half)) for p in range(share) for i in range(2)]
    scores = []
    for p, cols in items:
        k = k_s[p, :, cols]
        k = jnp.concatenate([jnp.where(low, k, zero), jnp.where(high, k, zero)], axis=0)
        scores.append(dot_t(q_s[p, :, cols], k))
    weights = []
    for s in scores:
        tops = [jnp.max(s[:, i * frames : (i + 1) * frames], axis=-1, keepdims=True) for i in range(2)]
        w = [jnp.exp2(s[:, i * frames : (i + 1) * frames] - tops[i]) for i in range(2)]
        weights.append(jnp.concatenate(w, axis=1).astype(jnp.bfloat16))
    parts = []
    for w, (p, cols) in zip(weights, items):
        v = v_s[p, :, cols]
        v = jnp.concatenate(
            [
                jnp.concatenate([jnp.where(low, v, zero), ones[0]], axis=1),
                jnp.concatenate([jnp.where(high, v, zero), ones[1]], axis=1),
            ],
            axis=0,
        )
        r = dot(w, v)
        parts.append(r[:, :half] / r[:, half:])
    a = [jnp.concatenate(parts[2 * p : 2 * p + 2], axis=1).astype(jnp.bfloat16) for p in range(share)]
    mixed = dot(jnp.concatenate(a, axis=0), wo_ref[...])
    for p in range(share):
        rows = pl.ds(p, frames, stride=share)
        put(a_s, rows, take(x_s, rows) + mixed[p * frames : (p + 1) * frames])
    for t in range(shards):
        for s in range(chips):
            outs[t][s] = take(a_s, pl.ds((t * chips + s) * block, block)).astype(jnp.bfloat16)


def temporal(own, came, gain, wq, wk, wv, wo, share, by_shard):
    shards, chips = len(own), len(came) + 1
    if not by_shard:
        shards, chips = chips, shards
    block, width = own[0].shape
    rows = block * chips * shards
    frames = rows // share
    return pl.pallas_call(
        functools.partial(temporal_kernel, chips, shards, share, by_shard),
        out_shape=[jax.ShapeDtypeStruct((chips, block, width), jnp.bfloat16)] * shards,
        scratch_shapes=[
            pltpu.VMEM((width // LANES, rows, LANES), jnp.float32),
            pltpu.VMEM((share, frames, width), jnp.bfloat16),
            pltpu.VMEM((share, frames, width), jnp.bfloat16),
            pltpu.VMEM((share, frames, width), jnp.bfloat16),
            pltpu.VMEM((width // LANES, rows, LANES), jnp.float32),
        ],
        compiler_params=pltpu.CompilerParams(vmem_limit_bytes=48 * 2**20),
        cost_estimate=cost(1.9),
        name="temporal",
    )(*own, *came, gain, wq, wk, wv, wo)


def assemble_kernel(turn, ids_ref, *refs):
    shards = len(refs) - 4
    pieces, (_, out_ref, held, sem) = refs[:shards], refs[shards:]
    chips, frames, step, _ = pieces[0].shape
    run = shards * step
    for z in range(shards):

        @pl.when(ids_ref[0] == z)
        def _():
            for s in range(chips):
                got = [pieces[mask(g ^ z, shards)][s].astype(jnp.float32) for g in range(shards)]
                held[pl.ds((s ^ ids_ref[1]) * frames, frames)] = jnp.concatenate(got, axis=1).astype(
                    jnp.bfloat16
                )

    copy = pltpu.make_async_copy(held, out_ref.at[:, pl.ds(turn * run, run), :], sem)
    copy.start()
    copy.wait()


def assemble(ids, pieces, whole, turn):
    shards = len(pieces)
    chips, frames, step, width = pieces[0].shape
    return pl.pallas_call(
        functools.partial(assemble_kernel, turn),
        in_specs=[pl.BlockSpec(memory_space=pltpu.SMEM)]
        + vmem(shards)
        + [pl.BlockSpec(memory_space=pl.ANY)],
        out_specs=pl.BlockSpec(memory_space=pl.ANY),
        out_shape=jax.ShapeDtypeStruct(whole.shape, whole.dtype),
        scratch_shapes=[
            pltpu.VMEM((chips * frames, shards * step, width), jnp.bfloat16),
            pltpu.SemaphoreType.DMA(()),
        ],
        input_output_aliases={shards + 1: 0},
        compiler_params=params(),
        cost_estimate=cost(60 if turn == 0 else 1),
        name="assemble",
    )(ids, *pieces, whole)


def blank(sizes):
    return pl.pallas_call(
        lambda out_ref: None,
        out_specs=pl.BlockSpec(memory_space=pl.ANY),
        out_shape=shape(*sizes),
        name="blank",
    )()


def swap(value, axis, size, mask):
    return lax.ppermute(value, axis, [(i, i ^ mask) for i in range(size)])


def shards_fn(
    shards,
    spots,
    latents,
    gain_one,
    query_one,
    key_one,
    value_one,
    out_one,
    gain_two,
    query_two,
    key_two,
    value_two,
    out_two,
):
    frames, local, width = latents.shape
    chips = spots // 2
    each = frames // chips
    share = local // shards
    turns = TURNS if share % (8 * TURNS) == 0 else 1
    zf = lax.axis_index("frame")
    chip = lax.axis_index("pos") // 2
    ids = jnp.stack([zf, chip]).astype(jnp.int32)
    row = lambda g: g.reshape(1, -1)

    over_shards = lambda v: [v[0]] + [swap(v[t], "frame", shards, mask(t, shards)) for t in range(1, shards)]
    over_chips = lambda v: [v[0]] + [swap(v[s], "pos", spots, 2 * s) for s in range(1, chips)]
    half = max(1, each // SPLIT)
    cut = lambda s, part: lax.dynamic_slice_in_dim(
        latents, (chip ^ s) * each + part * half, each - half if part else half, 0
    )
    early = [jnp.concatenate([cut(s, 0), latents[:1]], axis=0) for s in range(chips)]
    early = over_chips(early)
    late = over_chips([cut(s, 1) for s in range(chips)])
    found = jnp.stack([e[half] for e in early])
    hop = 1
    while hop < shards:
        sent = lax.ppermute(found, "frame", [(i, i + hop) for i in range(hop)])
        found = jnp.where((zf >= hop) & (zf < 2 * hop), sent, found)
        hop *= 2
    mine = [jnp.concatenate([e[:half], l], axis=0) for e, l in zip(early, late)]
    saved = spatial_ready(mine, row(gain_one), query_one, key_one, value_one, turns)
    rest = spatial_rest(
        swap(jnp.stack(mine), "pos", spots, 1), row(gain_one), key_one, value_one
    )
    found, ready = lax.optimization_barrier((found, saved))
    saved = (*saved, *rest)
    far = swap(found, "pos", spots, 1)
    mid, ends = spatial_first(
        ids, mine, found, far, row(gain_one), key_one, value_one, out_one, saved, shards, turns
    )
    saved = (*saved, *ends)
    step = share // turns
    flat = lambda v: [m.reshape(m.shape[0], each * step, width) for m in v]
    heads = lambda v: [m[0] for m in v]
    across = lambda v, n: [None] + [jnp.stack([m[i] for m in v]) for i in range(1, n)]
    whole = blank(latents.shape)
    weights = (row(gain_two), query_two, key_two, value_two, out_two)
    mids = [mid]
    for turn in range(1, turns):
        mids.append(spatial_later(ids, mine, saved, out_one, shards, turns, turn))
    pass
    got = [over_shards(mid) for mid in mids]
    done = None
    for turn in range(turns):
        now = got[turn]
        if turn + 1 < turns:
            more = got[turn + 1]
            now, mids[1] = lax.optimization_barrier((now, mids[1]))
        if turn:
            now, _ = lax.optimization_barrier((now, done))
        came = over_chips([None] + across(flat(now), chips)[1:])[1:]
        if turn + 1 < turns:
            came, _ = lax.optimization_barrier((came, more[1::2]))
        if turn:
            came, done = lax.optimization_barrier((came, done))
        done = temporal(heads(flat(now)), came, *weights, step, True)
        back = over_shards(done)
        whole = assemble(ids, [d.reshape(chips, each, step, width) for d in back], whole, turn)
    return whole


def solution(mesh):
    return jax.shard_map(
        functools.partial(shards_fn, mesh.shape["frame"], mesh.shape["pos"]),
        mesh=mesh,
        in_specs=(P("frame", "pos", None), P(), P(), P(), P(), P(), P(), P(), P(), P(), P()),
        out_specs=P("frame", "pos", None),
        check_vma=False,
    )
```

```python
import functools

import jax
import jax.numpy as jnp
from jax import lax
from jax.experimental import pallas as pl
from jax.experimental.pallas import tpu as pltpu
from jax.sharding import PartitionSpec as P

HEADS = 4
LANES = 128
READY = 40
SPLIT = 8
LATER = 6.4
ROOM = 26 * 2**20
TURNS = 2
LOG2E = 1.4426950408889634


def normed(wide, gain):
    factor = lax.rsqrt(jnp.mean(wide * wide, axis=-1, keepdims=True) + 1e-06)
    return wide * factor * gain


def dot(left, right):
    return jnp.dot(left, right, preferred_element_type=jnp.float32)


def dot_t(left, right):
    return lax.dot_general(
        left, right, (((1,), (1,)), ((), ())), preferred_element_type=jnp.float32
    )


def project(pieces, gain_ref, wk_ref, wv_ref, k_ref, v_ref):
    frames, local, width = pieces[0].shape
    gain = gain_ref[...]
    normal = [normed(r.reshape(frames * local, width).astype(jnp.float32), gain) for r in pieces]
    short = [n.astype(jnp.bfloat16) for n in normal]
    for weight, out in ((wk_ref, k_ref), (wv_ref, v_ref)):
        for s, n in enumerate(short):
            got = dot(n, weight[...]).astype(jnp.bfloat16)
            out[:, s * local : (s + 1) * local, :] = got.reshape(frames, local, width)
    return [n.reshape(frames, local, width) for n in normal]


def mask(place, shards):
    return (shards - place) % shards


def pick(rows, chips, turns, turn):
    local = rows.shape[0] // chips
    run = local // turns
    return jnp.concatenate(
        [rows[s * local + turn * run : s * local + (turn + 1) * run] for s in range(chips)], axis=0
    )


def attend(turns, turn, zf, pieces, q_ref, k_refs, v_refs, wo_ref, outs, mid_s):
    chips = len(pieces)
    shards, step, width = len(outs), *outs[0].shape[2:]
    half = width // 2
    depth = width // HEADS
    rows = chips * shards * step
    frames = q_ref.shape[0]
    places = 2 * k_refs[0].shape[1]
    low = lax.broadcasted_iota(jnp.int32, (rows, half), 1) < depth
    ones = jnp.ones((2 * places, half), jnp.bfloat16)
    both = lambda refs, f, cols: jnp.concatenate(
        [refs[0][f, :, cols], refs[1][f, :, cols], refs[2][0, :, cols], refs[3][0, :, cols]], axis=0
    )
    together = max(1, min(frames, ROOM // (2 * (2 * rows) * (2 * places) * 6)))
    for start in range(0, frames, together):
        now = range(start, min(start + together, frames))
        items = [(f, slice(p * half, (p + 1) * half)) for f in now for p in range(2)]
        scores = []
        for f, cols in items:
            q = q_ref[f, turn * rows : (turn + 1) * rows, cols]
            zero = jnp.zeros_like(q)
            q = jnp.concatenate([jnp.where(low, q, zero), jnp.where(low, zero, q)], axis=0)
            scores.append(dot_t(q, both(k_refs, f, cols)))
        weights = [
            jnp.exp2(s - jnp.max(s, axis=-1, keepdims=True)).astype(jnp.bfloat16) for s in scores
        ]
        sums = []
        for w, (f, cols) in zip(weights, items):
            r = dot(w, jnp.concatenate([both(v_refs, f, cols), ones], axis=1))
            top = jnp.where(low, r[:rows, :half], r[rows:, :half])
            bottom = jnp.where(low, r[:rows, half:], r[rows:, half:])
            sums.append(top / bottom)
        for u, f in enumerate(now):
            a = jnp.concatenate(sums[2 * u : 2 * u + 2], axis=1).astype(jnp.bfloat16)
            x = jnp.concatenate([r[f].astype(jnp.float32) for r in pieces], axis=0)
            mid_s[f] = pick(x, chips, turns, turn) + dot(a, wo_ref[...])
    for f in range(frames):
        for t in range(shards):
            for s in range(chips):
                at = pl.multiple_of((s * shards + (mask(t, shards) ^ zf)) * step, step)
                outs[t][s, f] = mid_s[f, pl.ds(at, step), :].astype(jnp.bfloat16)


def ready_kernel(chips, turns, *refs):
    mine, (gain, wq, wk, wv, q_ref, k_ref, v_ref) = refs[:chips], refs[chips:]
    normal = project([r[...] for r in mine], gain, wk, wv, k_ref, v_ref)
    scale = (wq.shape[0] // HEADS) ** -0.5 * LOG2E
    for f in range(q_ref.shape[0]):
        n = jnp.concatenate([w[f] for w in normal], axis=0)
        n = jnp.concatenate([pick(n, chips, turns, j) for j in range(turns)], axis=0)
        q_ref[f] = (dot(n.astype(jnp.bfloat16), wq[...]) * scale).astype(jnp.bfloat16)


def rest_kernel(chips, other, gain, wk, wv, k_ref, v_ref):
    project([other[s] for s in range(chips)], gain, wk, wv, k_ref, v_ref)


def first_kernel(chips, shards, turns, ids_ref, *refs):
    mine, (near, far, gain, wk, wv, wo, q, k, v, ko, vo) = refs[:chips], refs[chips : chips + 11]
    outs, saved = refs[chips + 11 : chips + 11 + shards], refs[chips + 11 + shards :]
    kn, vn, kf, vf, mid_s = saved
    project([near[s : s + 1] for s in range(chips)], gain, wk, wv, kn, vn)
    project([far[s : s + 1] for s in range(chips)], gain, wk, wv, kf, vf)
    attend(turns, 0, ids_ref[0], mine, q, (k, ko, kn, kf), (v, vo, vn, vf), wo, outs, mid_s)


def later_kernel(chips, turns, turn, ids_ref, *refs):
    mine, (q, k, v, ko, vo, kn, vn, kf, vf, wo) = refs[:chips], refs[chips : chips + 10]
    keys, values, outs = (k, ko, kn, kf), (v, vo, vn, vf), refs[chips + 10 : -1]
    attend(turns, turn, ids_ref[0], mine, q, keys, values, wo, outs, refs[-1])


def vmem(count):
    return [pl.BlockSpec(memory_space=pltpu.VMEM)] * count


def cost(microseconds):
    return pl.CostEstimate(
        flops=int(microseconds * 1e9), bytes_accessed=int(microseconds * 3.6e6), transcendentals=0
    )


def params():
    return pltpu.CompilerParams(vmem_limit_bytes=40 * 2**20)


def shape(*sizes):
    return jax.ShapeDtypeStruct(sizes, jnp.bfloat16)


def spatial_ready(mine, gain, wq, wk, wv, turns):
    chips = len(mine)
    frames, local, width = mine[0].shape
    args = (*mine, gain, wq, wk, wv)
    keys = shape(frames, chips * local, width)
    return pl.pallas_call(
        functools.partial(ready_kernel, chips, turns),
        in_specs=vmem(len(args)),
        out_specs=vmem(3),
        out_shape=[shape(frames, chips * local, width), keys, keys],
        compiler_params=params(),
        cost_estimate=cost(READY),
        name="spatial_ready",
    )(*args)


def spatial_rest(other, gain, wk, wv):
    chips, frames, local, width = other.shape
    args = (other, gain, wk, wv)
    return pl.pallas_call(
        functools.partial(rest_kernel, chips),
        in_specs=vmem(len(args)),
        out_specs=vmem(2),
        out_shape=[shape(frames, chips * local, width)] * 2,
        compiler_params=params(),
        cost_estimate=cost(40),
        name="spatial_rest",
    )(*args)


def spatial_first(ids, mine, near, far, gain, wk, wv, wo, saved, shards, turns):
    chips = len(mine)
    frames, local, width = mine[0].shape
    step = local // shards // turns
    args = (*mine, near, far, gain, wk, wv, wo, *saved)
    out = [shape(chips, frames, step, width)] * shards + [shape(1, chips * local, width)] * 4
    got = pl.pallas_call(
        functools.partial(first_kernel, chips, shards, turns),
        in_specs=[pl.BlockSpec(memory_space=pltpu.SMEM)] + vmem(len(args)),
        out_specs=vmem(len(out)),
        out_shape=out,
        scratch_shapes=[pltpu.VMEM((frames, chips * shards * step, width), jnp.float32)],
        compiler_params=params(),
        cost_estimate=cost(6.5),
        name="spatial_first",
    )(ids, *args)
    return got[:shards], got[shards:]


def spatial_later(ids, mine, saved, wo, shards, turns, turn):
    chips = len(mine)
    frames, local, width = mine[0].shape
    step = local // shards // turns
    args = (*mine, *saved, wo)
    return pl.pallas_call(
        functools.partial(later_kernel, chips, turns, turn),
        in_specs=[pl.BlockSpec(memory_space=pltpu.SMEM)] + vmem(len(args)),
        out_specs=vmem(shards),
        out_shape=[shape(chips, frames, step, width)] * shards,
        scratch_shapes=[pltpu.VMEM((frames, chips * shards * step, width), jnp.float32)],
        compiler_params=params(),
        cost_estimate=cost(LATER),
        name="spatial_later",
    )(ids, *args)


def take(ref, rows):
    return jnp.concatenate([ref[i, rows, :] for i in range(ref.shape[0])], axis=1)


def put(ref, rows, value):
    for i in range(ref.shape[0]):
        ref[i, rows, :] = value[:, i * LANES : (i + 1) * LANES]


def temporal_kernel(chips, shards, share, by_shard, *refs):
    near, far = (shards, chips) if by_shard else (chips, shards)
    own, refs = refs[:near], refs[near:]
    came, refs = refs[: far - 1], refs[far - 1 :]
    gain_ref, wq_ref, wk_ref, wv_ref, wo_ref = refs[:5]
    outs = refs[5 : 5 + shards]
    x_s, q_s, k_s, v_s, a_s = refs[5 + shards :]
    width = wq_ref.shape[0]
    depth = width // HEADS
    half = width // 2
    block = own[0].shape[0]
    frames = block // share * chips * shards
    for t in range(shards):
        for s in range(chips):
            i, j = (t, s) if by_shard else (s, t)
            piece = own[i][...] if j == 0 else came[j - 1][i]
            put(x_s, pl.ds((t * chips + s) * block, block), piece.astype(jnp.float32))
    gain = gain_ref[...]
    n = [normed(take(x_s, pl.ds(p, frames, stride=share)), gain) for p in range(share)]
    n = jnp.concatenate([v.astype(jnp.bfloat16) for v in n], axis=0)
    q_s[...] = (dot(n, wq_ref[...]) * (depth**-0.5 * LOG2E)).astype(jnp.bfloat16).reshape(q_s.shape)
    k_s[...] = dot(n, wk_ref[...]).astype(jnp.bfloat16).reshape(k_s.shape)
    v_s[...] = dot(n, wv_ref[...]).astype(jnp.bfloat16).reshape(v_s.shape)
    lane = lax.broadcasted_iota(jnp.int32, (frames, half), 1)
    low, high = lane < depth, lane >= depth
    ones = [c.astype(jnp.float32).astype(jnp.bfloat16) for c in (low, high)]

    zero = jnp.zeros((frames, half), jnp.bfloat16)
    items = [(p, slice(i * half, (i + 1) * half)) for p in range(share) for i in range(2)]
    scores = []
    for p, cols in items:
        k = k_s[p, :, cols]
        k = jnp.concatenate([jnp.where(low, k, zero), jnp.where(high, k, zero)], axis=0)
        scores.append(dot_t(q_s[p, :, cols], k))
    weights = []
    for s in scores:
        tops = [jnp.max(s[:, i * frames : (i + 1) * frames], axis=-1, keepdims=True) for i in range(2)]
        w = [jnp.exp2(s[:, i * frames : (i + 1) * frames] - tops[i]) for i in range(2)]
        weights.append(jnp.concatenate(w, axis=1).astype(jnp.bfloat16))
    parts = []
    for w, (p, cols) in zip(weights, items):
        v = v_s[p, :, cols]
        v = jnp.concatenate(
            [
                jnp.concatenate([jnp.where(low, v, zero), ones[0]], axis=1),
                jnp.concatenate([jnp.where(high, v, zero), ones[1]], axis=1),
            ],
            axis=0,
        )
        r = dot(w, v)
        parts.append(r[:, :half] / r[:, half:])
    a = [jnp.concatenate(parts[2 * p : 2 * p + 2], axis=1).astype(jnp.bfloat16) for p in range(share)]
    mixed = dot(jnp.concatenate(a, axis=0), wo_ref[...])
    for p in range(share):
        rows = pl.ds(p, frames, stride=share)
        put(a_s, rows, take(x_s, rows) + mixed[p * frames : (p + 1) * frames])
    for t in range(shards):
        for s in range(chips):
            outs[t][s] = take(a_s, pl.ds((t * chips + s) * block, block)).astype(jnp.bfloat16)


def temporal(own, came, gain, wq, wk, wv, wo, share, by_shard):
    shards, chips = len(own), len(came) + 1
    if not by_shard:
        shards, chips = chips, shards
    block, width = own[0].shape
    rows = block * chips * shards
    frames = rows // share
    return pl.pallas_call(
        functools.partial(temporal_kernel, chips, shards, share, by_shard),
        out_shape=[jax.ShapeDtypeStruct((chips, block, width), jnp.bfloat16)] * shards,
        scratch_shapes=[
            pltpu.VMEM((width // LANES, rows, LANES), jnp.float32),
            pltpu.VMEM((share, frames, width), jnp.bfloat16),
            pltpu.VMEM((share, frames, width), jnp.bfloat16),
            pltpu.VMEM((share, frames, width), jnp.bfloat16),
            pltpu.VMEM((width // LANES, rows, LANES), jnp.float32),
        ],
        compiler_params=pltpu.CompilerParams(vmem_limit_bytes=48 * 2**20),
        cost_estimate=cost(1.9),
        name="temporal",
    )(*own, *came, gain, wq, wk, wv, wo)


def assemble_kernel(turn, ids_ref, *refs):
    shards = len(refs) - 4
    pieces, (_, out_ref, held, sem) = refs[:shards], refs[shards:]
    chips, frames, step, _ = pieces[0].shape
    run = shards * step

    def put_back(s):
        at = pl.ds((s ^ ids_ref[1]) * frames, frames)
        return pltpu.make_async_copy(
            held.at[s], out_ref.at[at, pl.ds(turn * run, run), :], sem.at[s]
        )

    for z in range(shards):

        @pl.when(ids_ref[0] == z)
        def _():
            for s in range(chips):
                got = [pieces[mask(g ^ z, shards)][s].astype(jnp.float32) for g in range(shards)]
                held[s] = jnp.concatenate(got, axis=1).astype(jnp.bfloat16)
                put_back(s).start()

    for s in range(chips):
        put_back(s).wait()


def assemble(ids, pieces, whole, turn):
    shards = len(pieces)
    chips, frames, step, width = pieces[0].shape
    return pl.pallas_call(
        functools.partial(assemble_kernel, turn),
        in_specs=[pl.BlockSpec(memory_space=pltpu.SMEM)]
        + vmem(shards)
        + [pl.BlockSpec(memory_space=pl.ANY)],
        out_specs=pl.BlockSpec(memory_space=pl.ANY),
        out_shape=jax.ShapeDtypeStruct(whole.shape, whole.dtype),
        scratch_shapes=[
            pltpu.VMEM((chips, frames, shards * step, width), jnp.bfloat16),
            pltpu.SemaphoreType.DMA((chips,)),
        ],
        input_output_aliases={shards + 1: 0},
        compiler_params=params(),
        cost_estimate=cost(60 if turn == 0 else 1),
        name="assemble",
    )(ids, *pieces, whole)


def blank(sizes):
    return pl.pallas_call(
        lambda out_ref: None,
        out_specs=pl.BlockSpec(memory_space=pl.ANY),
        out_shape=shape(*sizes),
        name="blank",
    )()


def swap(value, axis, size, mask):
    return lax.ppermute(value, axis, [(i, i ^ mask) for i in range(size)])


def shards_fn(
    shards,
    spots,
    latents,
    gain_one,
    query_one,
    key_one,
    value_one,
    out_one,
    gain_two,
    query_two,
    key_two,
    value_two,
    out_two,
):
    frames, local, width = latents.shape
    chips = spots // 2
    each = frames // chips
    share = local // shards
    turns = TURNS if share % (8 * TURNS) == 0 else 1
    zf = lax.axis_index("frame")
    chip = lax.axis_index("pos") // 2
    ids = jnp.stack([zf, chip]).astype(jnp.int32)
    row = lambda g: g.reshape(1, -1)

    over_shards = lambda v: [v[0]] + [swap(v[t], "frame", shards, mask(t, shards)) for t in range(1, shards)]
    over_chips = lambda v: [v[0]] + [swap(v[s], "pos", spots, 2 * s) for s in range(1, chips)]
    half = max(1, each // SPLIT)
    cut = lambda s, part: lax.dynamic_slice_in_dim(
        latents, (chip ^ s) * each + part * half, each - half if part else half, 0
    )
    early = [jnp.concatenate([cut(s, 0), latents[:1]], axis=0) for s in range(chips)]
    early = over_chips(early)
    late = over_chips([cut(s, 1) for s in range(chips)])
    found = jnp.stack([e[half] for e in early])
    hop = 1
    while hop < shards:
        sent = lax.ppermute(found, "frame", [(i, i + hop) for i in range(hop)])
        found = jnp.where((zf >= hop) & (zf < 2 * hop), sent, found)
        hop *= 2
    mine = [jnp.concatenate([e[:half], l], axis=0) for e, l in zip(early, late)]
    saved = spatial_ready(mine, row(gain_one), query_one, key_one, value_one, turns)
    rest = spatial_rest(
        swap(jnp.stack(mine), "pos", spots, 1), row(gain_one), key_one, value_one
    )
    found, ready = lax.optimization_barrier((found, saved))
    saved = (*saved, *rest)
    far = swap(found, "pos", spots, 1)
    mid, ends = spatial_first(
        ids, mine, found, far, row(gain_one), key_one, value_one, out_one, saved, shards, turns
    )
    saved = (*saved, *ends)
    step = share // turns
    flat = lambda v: [m.reshape(m.shape[0], each * step, width) for m in v]
    heads = lambda v: [m[0] for m in v]
    across = lambda v, n: [None] + [jnp.stack([m[i] for m in v]) for i in range(1, n)]
    whole = blank(latents.shape)
    weights = (row(gain_two), query_two, key_two, value_two, out_two)
    mids = [mid]
    for turn in range(1, turns):
        mids.append(spatial_later(ids, mine, saved, out_one, shards, turns, turn))
    pass
    got = [over_shards(mid) for mid in mids]
    done = None
    for turn in range(turns):
        now = got[turn]
        if turn + 1 < turns:
            more = got[turn + 1]
            now, mids[1] = lax.optimization_barrier((now, mids[1]))
        if turn:
            now, _ = lax.optimization_barrier((now, done))
        came = over_chips([None] + across(flat(now), chips)[1:])[1:]
        if turn + 1 < turns:
            came, _ = lax.optimization_barrier((came, more[1::2]))
        if turn:
            came, done = lax.optimization_barrier((came, done))
        done = temporal(heads(flat(now)), came, *weights, step, True)
        back = over_shards(done)
        whole = assemble(ids, [d.reshape(chips, each, step, width) for d in back], whole, turn)
    return whole


def solution(mesh):
    return jax.shard_map(
        functools.partial(shards_fn, mesh.shape["frame"], mesh.shape["pos"]),
        mesh=mesh,
        in_specs=(P("frame", "pos", None), P(), P(), P(), P(), P(), P(), P(), P(), P(), P()),
        out_specs=P("frame", "pos", None),
        check_vma=False,
    )
```
